32 devices in a mesh: groups: 2 (over y), rows: 16 (over z, x, core).
Axes of the slice: x: 2, y: 2, z: 4, core: 2. Of those that a mesh axis runs over, the one named last changes fastest.
Arguments:
- tile_values: bfloat16 [3072, 256, 256], P(('groups', 'rows')), parts along dimension 0, may hold values from -0.078125 to 0.078125
- tile_rows: int32 [3072], P(('groups', 'rows')), parts along dimension 0, may hold values from 0 to 7
- tile_slots: int32 [3072], P(('groups', 'rows')), parts along dimension 0, may hold values from 0 to 255, as said below
- send_list: int32 [32, 16, 16], P(('groups', 'rows')), parts along dimension 0, may hold values from 0 to 7, as said below
- self_links: float32 [65536], P(('groups', 'rows')), parts along dimension 0, may hold values from 0.25 to 2
- start_panel: float32 [32, 65536], P(None, ('groups', 'rows')), parts along dimension 1, may hold values from -25 to 25
Outputs:
- next_basis: float32 [32, 65536], P(None, ('groups', 'rows')), parts along dimension 1
- couplings: float32 [4, 32, 32], P('groups'), parts along dimension 0
- factors: float32 [4, 32, 32], P('groups'), parts along dimension 0
The draws below stay inside these ranges and needn't reach their ends.
There are 2 independent parts, one for each index of `groups`. The reference program is written for one: setup_inputs(seed, part) draws one part's arguments, and reference() takes and returns one part's arrays. A program takes and returns all parts, laid end to end along the dimension named above; each array names one. Nothing has to cross between parts.
Inputs may be any that keep to these rules, and one draw needn't show every extreme that they name: send_list[p, q, s] is the local block of sender p that goes to receiver q in slot s. Each receiver gets 16 blocks from 4 senders, 8 blocks (slots below 8) from another 16/4, and none from the rest; slots at or past that number hold 0. tile_slots[t] = p * 16 + s names a live slot (p, s) of the tile's device; every live slot of a device is named by exactly one of its 96 tiles.
All inputs are finite; a program needn't handle non-finite values.
Results may differ from the reference program's by a relative error of at most 0.0042.
Values may be sent and summed in bfloat16 or wider, within the bound.
No kernel may reach another device: no remote copies, remote signals or barrier semaphores. Data moves between devices by JAX's collectives and lax.ppermute only.
A program may use at most 128 MiB of HBM per device.

```python
import math
import jax
import jax.numpy as jnp
from jax import lax

K = 32
TB = 256
BR = 8
ITERS = 2
TILES = 96
CAP = 16
ROWS = 32768
N_ROWS = 16


def slot_counts(key):
    key_list = jax.random.split(key, N_ROWS)
    shuffles = jax.vmap(lambda single: jax.random.permutation(single, N_ROWS))(key_list)
    row_rank = jnp.argsort(shuffles, axis=1)
    quarter = N_ROWS // 4
    return jnp.where(row_rank < quarter, CAP, jnp.where(row_rank < 2 * quarter, CAP // 2, 0)).astype(jnp.int32)


def draw_send_list(key, part):
    counts = slot_counts(key)
    key = jax.random.fold_in(key, 11)
    chosen = jax.random.randint(key, (N_ROWS, N_ROWS, CAP), 0, BR)
    filled = jnp.arange(CAP)[None, None, :] < counts.T[:, :, None]
    return jnp.where(filled, chosen, 0).astype(jnp.int32)


def draw_tile_slots(key, part):
    counts = slot_counts(key)
    key = jax.random.fold_in(key, 23)
    filled = (jnp.arange(CAP)[None, None, :] < counts[:, :, None]).reshape(N_ROWS, N_ROWS * CAP)
    ordering = jnp.argsort(jnp.where(filled, 0, 1).astype(jnp.int32), axis=1, stable=True)[:, :TILES]
    key_list = jax.random.split(key, N_ROWS)
    shuffles = jax.vmap(lambda single: jax.random.permutation(single, TILES))(key_list)
    mixed_order = jnp.take_along_axis(ordering, shuffles, axis=1)
    return mixed_order.reshape(-1).astype(jnp.int32)


def draw_start_panel(key, part):
    key = jax.random.fold_in(key, 37)
    first_key, second_key = jax.random.split(key, 2)
    position = jnp.arange(ROWS, dtype=jnp.float32)
    rising = 1.0 + 2.0 * position / ROWS
    spread = jax.random.truncated_normal(first_key, -4.0, 4.0, (K, ROWS), jnp.float32)
    rough = jnp.exp(jax.random.uniform(second_key, (K, ROWS), jnp.float32, -0.7, 0.7))
    values_out = spread * rising[None, :] * rough
    return values_out.astype(jnp.float32)


def touch_ends(drawn, rng, smallest, top_value):
    shape = drawn.shape
    place = [jax.random.randint(jax.random.fold_in(rng, axis), (), 0, shape[axis]) for axis in range(len(shape))]
    drawn = drawn.at[tuple(place)].set(smallest)
    longest = shape.index(max(shape))
    place[longest] = (place[longest] + 1) % shape[longest]
    return drawn.at[tuple(place)].set(top_value)


def shard_levels(stream_key, extent, pieces, low, top_value):
    factor_of = 1.0
    for dim, parts in pieces:
        heights = jax.random.uniform(jax.random.fold_in(jax.random.fold_in(stream_key, 6), dim), (parts,), jnp.float32, low / len(pieces), top_value / len(pieces))
        factor_of = factor_of * jnp.repeat(jnp.exp(heights), extent[dim] // parts).reshape((-1,) + (1,) * (len(extent) - 1 - dim))
    return factor_of


def noise(own_key, shape, width, limit, shards=(), held_as=jnp.bfloat16):
    factor_of = shard_levels(own_key, shape, shards, -0.22, 0.18) if shards else 1.0
    array = jax.random.normal(own_key, shape, jnp.float32) * width * factor_of
    return jnp.minimum(jnp.maximum(array, -limit), limit).astype(held_as)


def setup_inputs(seed: int = 0, part: int = 0) -> dict:
    arg_keys = jax.random.split(jax.random.key(seed), 7)
    part_splits = jax.random.split(jax.random.fold_in(arg_keys[6], part), 7)
    return {
        "tile_values": noise(part_splits[0], (N_ROWS * TILES, TB, TB), (24 * TB) ** -0.5, 0.078125, ((0, 16),)),
        "tile_rows": touch_ends(jax.random.randint(part_splits[1], (N_ROWS * TILES,), 0, BR), jax.random.fold_in(part_splits[1], 1), 0, BR - 1).astype(jnp.int32),
        "tile_slots": draw_tile_slots(jax.random.fold_in(jax.random.fold_in(arg_keys[6], part), 71), part),
        "send_list": draw_send_list(jax.random.fold_in(jax.random.fold_in(arg_keys[6], part), 71), part),
        "self_links": jnp.clip(jnp.exp(math.log(2.0) - 2.0794415 * jax.random.uniform(part_splits[4], (ROWS,), jnp.float32) ** shard_levels(part_splits[4], (ROWS,), ((0, 16),), -0.2, 0.2)), 0.25, 2.0),
        "start_panel": draw_start_panel(jax.random.fold_in(jax.random.fold_in(arg_keys[6], part), 71), part),
    }


precise = lax.Precision.HIGHEST

def product(left, right):
    return jnp.dot(left.astype(jnp.float32), right.astype(jnp.float32), precision=precise, preferred_element_type=jnp.float32)

def apply_operator(basis_now, self_links, tile_values, tile_rows, tile_slots, send_list):
    rounded = lax.optimization_barrier(basis_now.astype(jnp.bfloat16))
    blocks = rounded.astype(jnp.float32).reshape(K, N_ROWS * BR, TB).transpose(1, 0, 2)
    tile_groups = tile_values.reshape(N_ROWS, TILES, TB, TB)
    row_groups = tile_rows.reshape(N_ROWS, TILES)
    slot_groups = tile_slots.reshape(N_ROWS, TILES)

    def one_device(accumulated, inputs):
        device, tiles_here, rows_here, slots_here = inputs
        sender = (slots_here // CAP).astype(jnp.int32)
        within = (slots_here % CAP).astype(jnp.int32)
        col_index = (sender * BR + send_list[sender, device, within]).astype(jnp.int32)
        row_index = (device * BR + rows_here).astype(jnp.int32)
        weights = tiles_here.astype(jnp.float32)
        forward = jnp.einsum('tki,tji->tkj', blocks[col_index], weights, precision=precise)
        backward = jnp.einsum('tkj,tji->tki', blocks[row_index], weights, precision=precise)
        accumulated = accumulated.at[row_index].add(forward).at[col_index].add(backward)
        return (accumulated, None)
    start = jnp.zeros((N_ROWS * BR, K, TB), jnp.float32)
    devices = jnp.arange(N_ROWS, dtype=jnp.int32)
    accumulated, unused = lax.scan(one_device, start, (devices, tile_groups, row_groups, slot_groups))
    coupled = accumulated.transpose(1, 0, 2).reshape(K, N_ROWS * BR * TB)
    return self_links[None, :] * basis_now + coupled

def reference(tile_values, tile_rows, tile_slots, send_list, self_links, start_panel):
    gram_now = product(start_panel, start_panel.T)
    factor = jnp.linalg.cholesky(gram_now)
    basis_now = jax.scipy.linalg.solve_triangular(factor, start_panel, lower=True)
    basis_prev = jnp.zeros_like(basis_now)
    factor_prev = jnp.zeros((K, K), jnp.float32)
    couplings = []
    factors = []
    for iteration in range(ITERS):
        applied = apply_operator(basis_now, self_links, tile_values, tile_rows, tile_slots, send_list)
        coupling = product(basis_now, applied.T)
        residual = applied - product(coupling.T, basis_now) - product(factor_prev.T, basis_prev)
        gram_now = product(residual, residual.T)
        factor = jnp.linalg.cholesky(gram_now)
        following = jax.scipy.linalg.solve_triangular(factor, residual, lower=True)
        couplings.append(coupling)
        factors.append(factor)
        basis_prev, basis_now, factor_prev = (basis_now, following, factor)
    return (basis_now * math.sqrt(ROWS), jnp.stack(couplings), jnp.stack(factors))
```

```python
import functools
import math

import jax
import jax.numpy as jnp
import numpy as np
from jax import lax
from jax.experimental import pallas as pl
from jax.experimental.pallas import tpu as pltpu
from jax.sharding import PartitionSpec as P

precise = lax.Precision.HIGHEST
SMEM = pl.BlockSpec(memory_space=pltpu.SMEM)
VMEM = pl.BlockSpec(memory_space=pltpu.VMEM)
UNROLL = 16


def product(left, right):
    return lax.dot_general(left, right, (((1,), (0,)), ((), ())), precision=precise, preferred_element_type=jnp.float32)


def product_t(left, right):
    return lax.dot_general(left, right, (((1,), (1,)), ((), ())), precision=precise, preferred_element_type=jnp.float32)


def t_product(left, right):
    return lax.dot_general(left, right, (((0,), (0,)), ((), ())), precision=precise, preferred_element_type=jnp.float32)


def swap(array, offset):
    count = lax.axis_size("rows")
    return lax.ppermute(array, "rows", [(place, place ^ offset) for place in range(count)])


def stages(count):
    bits = count.bit_length() - 1
    top = min(2, bits)
    return list(range(bits - top)), bits - top, 1 << top


def positions(count):
    low, shift, wide = stages(count)
    bits = count.bit_length() - 1
    place = []
    for offset in range(count):
        spot = offset >> shift
        for bit in low:
            spot += ((offset >> bit) & 1) << (bits - 1 - bit)
        place.append(spot)
    return np.array(place, np.int32)


def gather_panel(panel):
    low, shift, wide = stages(lax.axis_size("rows"))
    arrays = [jnp.stack([panel] + [swap(panel, far << shift) for far in range(1, wide)])]
    for bit in reversed(low):
        arrays = arrays + [swap(array, 1 << bit) for array in arrays]
    return arrays


def reduce_panels(kept, sent):
    low, shift, wide = stages(lax.axis_size("rows"))
    for bit in low:
        arrived = swap(sent, 1 << bit)
        half = kept.shape[0] // 2
        if bit != low[-1]:
            sent = (kept[half:] + arrived[half:]).astype(jnp.bfloat16)
            kept = kept[:half] + arrived[:half]
    terms = []
    for far in range(wide - 1, 0, -1):
        terms.append(swap((kept[far] + arrived[far]).astype(jnp.bfloat16), far << shift))
    return [kept[0], arrived[0]] + terms


def reduce_small(array):
    low, shift, wide = stages(lax.axis_size("rows"))
    for bit in low:
        array = array + swap(array, 1 << bit)
    others = [swap(array, far << shift) for far in range(1, wide)]
    total = array + others[0]
    if wide == 4:
        total = total + (others[1] + others[2])
    return total


def tile_place(tile, me_ref, rows_ref, slots_ref, list_ref, place_ref, capacity, tile_size):
    slot = slots_ref[tile]
    block = list_ref[slot]
    piece = place_ref[(slot // capacity) ^ me_ref[0]]
    own = pl.ds(pl.multiple_of(rows_ref[tile] * tile_size, tile_size), tile_size)
    other = pl.ds(pl.multiple_of(block * tile_size, tile_size), tile_size)
    return own, piece, other


def backward_kernel(me_ref, rows_ref, slots_ref, list_ref, place_ref, high_ref, low_ref, tiles_ref, kept_ref, sent_ref, total, *, capacity):
    tiles, tile_size, _ = tiles_ref.shape
    width = high_ref.shape[0]
    half = kept_ref.shape[0]
    total[...] = jnp.zeros_like(total)

    def some(step, carry):
        for u in range(UNROLL):
            tile = step * UNROLL + u
            own, piece, other = tile_place(tile, me_ref, rows_ref, slots_ref, list_ref, place_ref, capacity, tile_size)
            left = jnp.concatenate([high_ref[:, own], low_ref[:, own]], axis=0)
            both = jnp.dot(left, tiles_ref[tile], preferred_element_type=jnp.float32)
            total[piece, :, other] += (both[:width] + both[width:]).astype(total.dtype)
        return carry

    lax.fori_loop(0, tiles // UNROLL, some, 0)
    kept_ref[...] = total[:half].astype(kept_ref.dtype)
    sent_ref[...] = total[half:].astype(sent_ref.dtype)


def forward_kernel(me_ref, rows_ref, slots_ref, list_ref, place_ref, tiles_ref, *refs, capacity, groups):
    group_refs, (out_ref, pieces) = refs[:groups], refs[groups:]
    tiles, tile_size, _ = tiles_ref.shape
    wide = group_refs[0].shape[0]
    for group, ref in enumerate(group_refs):
        pieces[group * wide : (group + 1) * wide] = ref[...]
    out_ref[...] = jnp.zeros_like(out_ref)

    def some(step, carry):
        for u in range(UNROLL):
            tile = step * UNROLL + u
            own, piece, other = tile_place(tile, me_ref, rows_ref, slots_ref, list_ref, place_ref, capacity, tile_size)
            out_ref[:, own] += lax.dot_general(
                pieces[piece, :, other], tiles_ref[tile], (((1,), (1,)), ((), ())), preferred_element_type=jnp.float32
            )
        return carry

    lax.fori_loop(0, tiles // UNROLL, some, 0)


def split_kernel(whole_ref, high_ref, low_ref):
    high = whole_ref[...].astype(jnp.bfloat16)
    high_ref[...] = high
    low_ref[...] = (whole_ref[...] - high.astype(jnp.float32)).astype(jnp.bfloat16)


def combine_kernel(links_ref, panel_ref, forward_ref, *refs):
    term_refs, (out_ref, high_ref, low_ref) = refs[:-3], refs[-3:]
    out = links_ref[...] * panel_ref[...] + forward_ref[...]
    for ref in term_refs:
        out = out + ref[...].astype(jnp.float32)
    out_ref[...] = out
    high = out.astype(jnp.bfloat16)
    high_ref[...] = high
    low_ref[...] = (out - high.astype(jnp.float32)).astype(jnp.bfloat16)


def gram_kernel(left_ref, right_ref, out_ref):
    both = jnp.concatenate([left_ref[...], right_ref[...]], axis=0)
    out_ref[...] = product_t(both, both)


def factor_of(gram):
    width = gram.shape[0]
    rows = lax.broadcasted_iota(jnp.int32, (width, width), 0)
    columns = lax.broadcasted_iota(jnp.int32, (width, width), 1)
    unit = (rows == columns).astype(jnp.float32)
    work = jnp.concatenate([gram, unit], axis=1)
    found = []
    for j in range(width):
        scale = lax.rsqrt(work[j : j + 1, j : j + 1])
        row = work[j : j + 1, :] * scale
        found.append(row)
        work = work - (work[:, j : j + 1] * scale) * row
    found = jnp.concatenate(found, axis=0)
    factor = jnp.where(rows >= columns, found[:, :width].T, 0.0)
    return factor, found[:, width:]


def first_coefficients_kernel(gram_ref, coupling_ref, factor_ref, mix_ref):
    width = gram_ref.shape[0] // 2
    gram = gram_ref[...]
    _, inverse0 = factor_of(gram[:width, :width])
    coupling = product_t(product(inverse0, gram[:width, width:]), inverse0)
    image = product_t(product(inverse0, gram[width:, width:]), inverse0)
    factor, inverse1 = factor_of(image - t_product(coupling, coupling))
    coupling_ref[...] = coupling
    factor_ref[...] = factor
    after = product(inverse1, inverse0)
    before = -product(inverse1, t_product(coupling, inverse0))
    none = jnp.zeros_like(after)
    mix_ref[...] = jnp.concatenate(
        [
            jnp.concatenate([inverse0, none, none], axis=1),
            jnp.concatenate([before, after, none], axis=1),
            jnp.concatenate([none, before, after], axis=1),
        ],
        axis=0,
    )


def basis_kernel(mix_ref, start_ref, first_ref, links_ref, forward_ref, *refs):
    term_refs, (basis_ref, gram_ref) = refs[:-2], refs[-2:]
    width = start_ref.shape[0]
    second = links_ref[...] * first_ref[...] + forward_ref[...]
    for ref in term_refs:
        second = second + ref[...].astype(jnp.float32)
    basis = product(mix_ref[...], jnp.concatenate([start_ref[...], first_ref[...], second], axis=0))
    basis_ref[...] = basis
    gram_ref[...] = product_t(basis, basis[2 * width :])


def last_kernel(gram_ref, factor_ref, basis_ref, out_ref, coupling_ref, last_ref, *, scale):
    width = gram_ref.shape[1]
    before = factor_ref[...]
    crossed, coupling, image = gram_ref[:width], gram_ref[width : 2 * width], gram_ref[2 * width :]
    mixed = t_product(crossed, before)
    gram = image - t_product(coupling, coupling) - mixed - mixed.T + t_product(before, before)
    factor, inverse = factor_of(gram)
    coupling_ref[...] = coupling
    last_ref[...] = factor
    terms = jnp.concatenate([-product(inverse, before.T), -product(inverse, coupling.T), inverse], axis=1)
    out_ref[...] = product(terms, basis_ref[...]) * scale


def call(kernel, out, *args, name, scratch=(), specs=None, cost=None):
    return pl.pallas_call(
        kernel,
        out_shape=out,
        in_specs=specs or [VMEM] * len(args),
        out_specs=jax.tree.map(lambda _: VMEM, out),
        scratch_shapes=list(scratch),
        compiler_params=pltpu.CompilerParams(vmem_limit_bytes=40 << 20),
        cost_estimate=cost,
        name=name,
    )(*args)


def on_device(tile_values, tile_rows, tile_slots, send_list, self_links, start_panel):
    count = lax.axis_size("rows")
    width, here = start_panel.shape
    tiles, tile_size, _ = tile_values.shape
    capacity = send_list.shape[2]
    f32, bf16 = jnp.float32, jnp.bfloat16
    shape = jax.ShapeDtypeStruct
    links = self_links[None, :]
    place = jnp.asarray(positions(count))
    me = lax.axis_index("rows").astype(jnp.int32).reshape(1)
    listed = lax.all_to_all(send_list[0], "rows", split_axis=0, concat_axis=0, tiled=True).reshape(-1)
    indices = (me, tile_rows, tile_slots, listed, place)
    spec = [SMEM] * len(indices)
    work = 2 * tiles * width * tile_size * tile_size
    cost = pl.CostEstimate(flops=4 * work, bytes_accessed=2 * tile_values.size, transcendentals=0)
    total_type = f32 if count <= 16 else bf16

    def backward(high, low):
        return call(
            functools.partial(backward_kernel, capacity=capacity),
            (shape((count // 2, width, here), f32 if count <= 16 else bf16), shape((count // 2, width, here), bf16)),
            *indices, high, low, tile_values,
            name="backward", specs=spec + [VMEM] * 3, scratch=[pltpu.VMEM((count, width, here), total_type)], cost=cost,
        )

    def forward(groups):
        return call(
            functools.partial(forward_kernel, capacity=capacity, groups=len(groups)),
            shape((width, here), f32),
            *indices, tile_values, *groups,
            name="forward", specs=spec + [VMEM] * (1 + len(groups)),
            scratch=[pltpu.VMEM((count, width, here), bf16)], cost=cost,
        )

    def applied(high, low):
        groups = gather_panel(high)
        kept, sent = backward(high, low)
        terms = reduce_panels(kept, sent)
        return [forward(groups)] + terms

    panel = shape((width, here), f32)
    half = shape((width, here), bf16)
    small = shape((width, width), f32)
    high, low = call(split_kernel, (half, half), start_panel, name="split")
    terms = applied(high, low)
    first, high, low = call(combine_kernel, (panel, half, half), links, start_panel, *terms, name="combine")
    gram = call(gram_kernel, shape((2 * width, 2 * width), f32), start_panel, first, name="gram")
    gram = reduce_small(gram)
    coupling1, factor1, mix = call(
        first_coefficients_kernel, (small, small, shape((3 * width, 3 * width), f32)), gram, name="coefficients"
    )
    terms = applied(high, low)
    basis, gram = call(
        basis_kernel, (shape((3 * width, here), f32), shape((3 * width, width), f32)), mix, start_panel, first, links, *terms, name="basis"
    )
    gram = reduce_small(gram)
    out, coupling2, factor2 = call(
        functools.partial(last_kernel, scale=math.sqrt(here * count)), (panel, small, small), gram, factor1, basis, name="last"
    )
    return out, jnp.stack([coupling1, coupling2]), jnp.stack([factor1, factor2])


def solution(mesh):
    placed = (
        P(("groups", "rows"), None, None),
        P(("groups", "rows")),
        P(("groups", "rows")),
        P(("groups", "rows"), None, None),
        P(("groups", "rows")),
        P(None, ("groups", "rows")),
    )
    return jax.shard_map(
        on_device,
        mesh=mesh,
        in_specs=placed,
        out_specs=(P(None, ("groups", "rows")), P("groups", None, None), P("groups", None, None)),
        check_vma=False,
    )
```

```python
import functools
import math

import jax
import jax.numpy as jnp
import numpy as np
from jax import lax
from jax.experimental import pallas as pl
from jax.experimental.pallas import tpu as pltpu
from jax.sharding import PartitionSpec as P

precise = lax.Precision.HIGHEST
SMEM = pl.BlockSpec(memory_space=pltpu.SMEM)
VMEM = pl.BlockSpec(memory_space=pltpu.VMEM)
ANY = pl.BlockSpec(memory_space=pl.ANY)
UNROLL = 16


def product(left, right):
    return lax.dot_general(left, right, (((1,), (0,)), ((), ())), precision=precise, preferred_element_type=jnp.float32)


def product_t(left, right):
    return lax.dot_general(left, right, (((1,), (1,)), ((), ())), precision=precise, preferred_element_type=jnp.float32)


def t_product(left, right):
    return lax.dot_general(left, right, (((0,), (0,)), ((), ())), precision=precise, preferred_element_type=jnp.float32)


def swap(array, offset):
    count = lax.axis_size("rows")
    return lax.ppermute(array, "rows", [(place, place ^ offset) for place in range(count)])


def stages(count):
    bits = count.bit_length() - 1
    top = min(2, bits)
    return list(range(bits - top)), bits - top, 1 << top


def positions(count):
    low, shift, wide = stages(count)
    bits = count.bit_length() - 1
    place = []
    for offset in range(count):
        spot = offset >> shift
        for bit in low:
            spot += ((offset >> bit) & 1) << (bits - 1 - bit)
        place.append(spot)
    return np.array(place, np.int32)


def gather_panel(panel):
    low, shift, wide = stages(lax.axis_size("rows"))
    return [panel] + [swap(panel, far << shift) for far in range(1, wide)]


def spread_panels(pieces, token):
    low, shift, wide = stages(lax.axis_size("rows"))
    step = max(1, wide // 2)
    arrays = [stacked(pieces[at : at + step], token) for at in range(0, wide, step)]
    for bit in reversed(low):
        arrays = arrays + [swap(array, 1 << bit) for array in arrays]
    return arrays


def reduce_panels(kept, sent):
    low, shift, wide = stages(lax.axis_size("rows"))
    for bit in low[:-1]:
        arrived = swap(sent, 1 << bit)
        half = kept.shape[0] // 2
        kept, sent = added(kept, arrived)
    near, far = sent[: wide // 2], sent[wide // 2 :]
    arrived = [swap(far, 1 << low[-1]), swap(near, 1 << low[-1])]
    return kept, arrived


def finish_panels(kept, arrived):
    low, shift, wide = stages(lax.axis_size("rows"))
    far, near = arrived
    terms = []
    for place in range(wide - 1, 0, -1):
        part = far[place - wide // 2] if place >= wide // 2 else near[place]
        terms.append(swap((kept[place] + part).astype(jnp.bfloat16), place << shift))
    return [kept[0], near[0]] + terms


def added_kernel(kept_ref, arrived_ref, near_ref, far_ref):
    half = near_ref.shape[0]
    near_ref[...] = kept_ref[:half] + arrived_ref[:half].astype(jnp.float32)
    far_ref[...] = (kept_ref[half:] + arrived_ref[half:].astype(jnp.float32)).astype(jnp.bfloat16)


def added(kept, arrived):
    half, width, here = kept.shape[0] // 2, *kept.shape[1:]
    shape = jax.ShapeDtypeStruct
    return call(added_kernel, (shape((half, width, here), jnp.float32), shape((half, width, here), jnp.bfloat16)), kept, arrived, name="added")


def stacked_kernel(*refs):
    for index, ref in enumerate(refs[:-2]):
        refs[-1][index] = ref[...]


def stacked(pieces, token):
    out = jax.ShapeDtypeStruct((len(pieces), *pieces[0].shape), pieces[0].dtype)
    return call(stacked_kernel, out, *pieces, token, name="stacked", specs=[VMEM] * len(pieces) + [ANY])


def reduce_small(array):
    low, shift, wide = stages(lax.axis_size("rows"))
    for bit in low:
        array = array + swap(array, 1 << bit)
    others = [swap(array, far << shift) for far in range(1, wide)]
    total = array + others[0]
    if wide == 4:
        total = total + (others[1] + others[2])
    return total


def tile_place(tile, me_ref, rows_ref, slots_ref, list_ref, place_ref, capacity, tile_size):
    slot = slots_ref[tile]
    block = list_ref[slot]
    piece = place_ref[(slot // capacity) ^ me_ref[0]]
    own = pl.ds(pl.multiple_of(rows_ref[tile] * tile_size, tile_size), tile_size)
    other = pl.ds(pl.multiple_of(block * tile_size, tile_size), tile_size)
    return own, piece, other


def backward_kernel(me_ref, rows_ref, slots_ref, list_ref, place_ref, high_ref, low_ref, tiles_ref, kept_ref, sent_ref, total, *, capacity):
    tiles, tile_size, _ = tiles_ref.shape
    width = high_ref.shape[0]
    half = kept_ref.shape[0]
    total[...] = jnp.zeros_like(total)

    def some(step, carry):
        for u in range(UNROLL):
            tile = step * UNROLL + u
            own, piece, other = tile_place(tile, me_ref, rows_ref, slots_ref, list_ref, place_ref, capacity, tile_size)
            left = jnp.concatenate([high_ref[:, own], low_ref[:, own]], axis=0)
            both = jnp.dot(left, tiles_ref[tile], preferred_element_type=jnp.float32)
            total[piece, :, other] += (both[:width] + both[width:]).astype(total.dtype)
        return carry

    lax.fori_loop(0, tiles // UNROLL, some, 0)
    kept_ref[...] = total[:half].astype(kept_ref.dtype)
    sent_ref[...] = total[half:].astype(sent_ref.dtype)


def forward_kernel(me_ref, rows_ref, slots_ref, list_ref, place_ref, tiles_ref, *refs, capacity, groups):
    group_refs, (out_ref, pieces) = refs[:groups], refs[groups:]
    tiles, tile_size, _ = tiles_ref.shape
    wide = group_refs[0].shape[0]
    for group, ref in enumerate(group_refs):
        pieces[group * wide : (group + 1) * wide] = ref[...]
    out_ref[...] = jnp.zeros_like(out_ref)

    def some(step, carry):
        for u in range(UNROLL):
            tile = step * UNROLL + u
            own, piece, other = tile_place(tile, me_ref, rows_ref, slots_ref, list_ref, place_ref, capacity, tile_size)
            out_ref[:, own] += lax.dot_general(
                pieces[piece, :, other], tiles_ref[tile], (((1,), (1,)), ((), ())), preferred_element_type=jnp.float32
            )
        return carry

    lax.fori_loop(0, tiles // UNROLL, some, 0)


def split_kernel(whole_ref, high_ref, low_ref):
    high = whole_ref[...].astype(jnp.bfloat16)
    high_ref[...] = high
    low_ref[...] = (whole_ref[...] - high.astype(jnp.float32)).astype(jnp.bfloat16)


def combine_kernel(links_ref, panel_ref, forward_ref, *refs):
    term_refs, (out_ref, high_ref, low_ref) = refs[:-3], refs[-3:]
    out = (links_ref[...] - 1.0) * panel_ref[...] + forward_ref[...]
    for ref in term_refs:
        out = out + ref[...].astype(jnp.float32)
    out_ref[...] = out
    high = out.astype(jnp.bfloat16)
    high_ref[...] = high
    low_ref[...] = (out - high.astype(jnp.float32)).astype(jnp.bfloat16)


def gram_kernel(left_ref, right_ref, token_ref, out_ref):
    both = jnp.concatenate([left_ref[...], right_ref[...]], axis=0)
    out_ref[...] = product_t(both, both)


def factor_of(gram):
    width = gram.shape[0]
    rows = lax.broadcasted_iota(jnp.int32, (width, width), 0)
    columns = lax.broadcasted_iota(jnp.int32, (width, width), 1)
    unit = (rows == columns).astype(jnp.float32)
    work = jnp.concatenate([gram, unit], axis=1)
    found = []
    for j in range(width):
        scale = lax.rsqrt(work[j : j + 1, j : j + 1])
        row = work[j : j + 1, :] * scale
        found.append(row)
        work = work - (work[:, j : j + 1] * scale) * row
    found = jnp.concatenate(found, axis=0)
    factor = jnp.where(rows >= columns, found[:, :width].T, 0.0)
    return factor, found[:, width:]


def first_coefficients_kernel(gram_ref, token_ref, coupling_ref, factor_ref, mix_ref):
    width = gram_ref.shape[0] // 2
    gram = gram_ref[...]
    _, inverse0 = factor_of(gram[:width, :width])
    coupling = product_t(product(inverse0, gram[:width, width:]), inverse0)
    image = product_t(product(inverse0, gram[width:, width:]), inverse0)
    factor, inverse1 = factor_of(image - t_product(coupling, coupling))
    rows = lax.broadcasted_iota(jnp.int32, (width, width), 0)
    columns = lax.broadcasted_iota(jnp.int32, (width, width), 1)
    coupling_ref[...] = coupling + (rows == columns).astype(jnp.float32)
    factor_ref[...] = factor
    after = product(inverse1, inverse0)
    before = -product(inverse1, t_product(coupling, inverse0))
    none = jnp.zeros_like(after)
    mix_ref[...] = jnp.concatenate(
        [
            jnp.concatenate([inverse0, none, none], axis=1),
            jnp.concatenate([before, after, none], axis=1),
            jnp.concatenate([before, before, after], axis=1),
        ],
        axis=0,
    )


def basis_kernel(mix_ref, start_ref, first_ref, links_ref, forward_ref, *refs):
    term_refs, (basis_ref, gram_ref) = refs[:-2], refs[-2:]
    width = start_ref.shape[0]
    second = links_ref[...] * first_ref[...] + forward_ref[...]
    for ref in term_refs:
        second = second + ref[...].astype(jnp.float32)
    basis = product(mix_ref[...], jnp.concatenate([start_ref[...], first_ref[...], second], axis=0))
    basis_ref[...] = basis
    gram_ref[...] = product_t(basis, basis[2 * width :])


def last_kernel(gram_ref, factor_ref, basis_ref, out_ref, coupling_ref, last_ref, *, scale):
    width = gram_ref.shape[1]
    before = factor_ref[...]
    crossed, coupling, image = gram_ref[:width], gram_ref[width : 2 * width], gram_ref[2 * width :]
    mixed = t_product(crossed, before)
    gram = image - t_product(coupling, coupling) - mixed - mixed.T + t_product(before, before)
    factor, inverse = factor_of(gram)
    coupling_ref[...] = coupling
    last_ref[...] = factor
    terms = jnp.concatenate([-product(inverse, before.T), -product(inverse, coupling.T), inverse], axis=1)
    out_ref[...] = product(terms, basis_ref[...]) * scale


def call(kernel, out, *args, name, scratch=(), specs=None, cost=None):
    return pl.pallas_call(
        kernel,
        out_shape=out,
        in_specs=specs or [VMEM] * len(args),
        out_specs=jax.tree.map(lambda _: VMEM, out),
        scratch_shapes=list(scratch),
        compiler_params=pltpu.CompilerParams(vmem_limit_bytes=22 << 20),
        cost_estimate=cost,
        name=name,
    )(*args)


def on_device(tile_values, tile_rows, tile_slots, send_list, self_links, start_panel):
    count = lax.axis_size("rows")
    width, here = start_panel.shape
    tiles, tile_size, _ = tile_values.shape
    capacity = send_list.shape[2]
    f32, bf16 = jnp.float32, jnp.bfloat16
    shape = jax.ShapeDtypeStruct
    links = self_links[None, :]
    place = jnp.asarray(positions(count))
    me = lax.axis_index("rows").astype(jnp.int32).reshape(1)
    listed = lax.all_to_all(send_list[0], "rows", split_axis=0, concat_axis=0, tiled=True).reshape(-1)
    indices = (me, tile_rows, tile_slots, listed, place)
    spec = [SMEM] * len(indices)
    work = 2 * tiles * width * tile_size * tile_size
    cost = pl.CostEstimate(flops=4 * work, bytes_accessed=2 * tile_values.size, transcendentals=0)
    total_type = f32 if count <= 16 else bf16

    def backward(high, low):
        return call(
            functools.partial(backward_kernel, capacity=capacity),
            (shape((count // 2, width, here), f32 if count <= 16 else bf16), shape((count // 2, width, here), bf16)),
            *indices, high, low, tile_values,
            name="backward", specs=spec + [VMEM] * 3, scratch=[pltpu.VMEM((count, width, here), total_type)], cost=cost,
        )

    def forward(groups):
        return call(
            functools.partial(forward_kernel, capacity=capacity, groups=len(groups)),
            shape((width, here), f32),
            *indices, tile_values, *groups,
            name="forward", specs=spec + [VMEM] * (1 + len(groups)),
            scratch=[pltpu.VMEM((count, width, here), bf16)], cost=cost,
        )

    def applied(high, low):
        pieces = gather_panel(high)
        kept, sent = backward(high, low)
        kept, arrived = reduce_panels(kept, sent)
        groups = spread_panels(pieces, arrived[1])
        terms = finish_panels(kept, arrived)
        return [forward(groups)] + terms, arrived[1]

    panel = shape((width, here), f32)
    half = shape((width, here), bf16)
    small = shape((width, width), f32)
    high, low = call(split_kernel, (half, half), start_panel, name="split")
    terms, _ = applied(high, low)
    first, high, low = call(combine_kernel, (panel, half, half), links, start_panel, *terms, name="combine")
    terms, token = applied(high, low)
    gram = call(gram_kernel, shape((2 * width, 2 * width), f32), start_panel, first, token, name="gram", specs=[VMEM, VMEM, ANY])
    gram = reduce_small(gram)
    coupling1, factor1, mix = call(
        first_coefficients_kernel, (small, small, shape((3 * width, 3 * width), f32)), gram, terms[0], name="coefficients", specs=[VMEM, ANY]
    )
    basis, gram = call(
        basis_kernel, (shape((3 * width, here), f32), shape((3 * width, width), f32)), mix, start_panel, first, links, *terms, name="basis"
    )
    gram = reduce_small(gram)
    out, coupling2, factor2 = call(
        functools.partial(last_kernel, scale=math.sqrt(here * count)), (panel, small, small), gram, factor1, basis, name="last"
    )
    return out, jnp.stack([coupling1, coupling2]), jnp.stack([factor1, factor2])


def solution(mesh):
    placed = (
        P(("groups", "rows"), None, None),
        P(("groups", "rows")),
        P(("groups", "rows")),
        P(("groups", "rows"), None, None),
        P(("groups", "rows")),
        P(None, ("groups", "rows")),
    )
    return jax.shard_map(
        on_device,
        mesh=mesh,
        in_specs=placed,
        out_specs=(P(None, ("groups", "rows")), P("groups", None, None), P("groups", None, None)),
        check_vma=False,
    )
```

```python
import functools
import math

import jax
import jax.numpy as jnp
import numpy as np
from jax import lax
from jax.experimental import pallas as pl
from jax.experimental.pallas import tpu as pltpu
from jax.sharding import PartitionSpec as P

precise = lax.Precision.HIGHEST
SMEM = pl.BlockSpec(memory_space=pltpu.SMEM)
VMEM = pl.BlockSpec(memory_space=pltpu.VMEM)
ANY = pl.BlockSpec(memory_space=pl.ANY)
UNROLL = 16
STEP = 16
ITERS = 2


def product(left, right):
    return lax.dot_general(left, right, (((1,), (0,)), ((), ())), precision=precise, preferred_element_type=jnp.float32)


def product_t(left, right):
    return lax.dot_general(left, right, (((1,), (1,)), ((), ())), precision=precise, preferred_element_type=jnp.float32)


def t_product(left, right):
    return lax.dot_general(left, right, (((0,), (0,)), ((), ())), precision=precise, preferred_element_type=jnp.float32)


def swap(array, offset):
    count = lax.axis_size("rows")
    return lax.ppermute(array, "rows", [(place, place ^ offset) for place in range(count)])


def stages(count):
    bits = count.bit_length() - 1
    top = min(2, bits)
    return list(range(bits - top)), bits - top, 1 << top


def positions(count):
    low, shift, wide = stages(count)
    bits = count.bit_length() - 1
    place = []
    for offset in range(count):
        spot = offset >> shift
        for bit in low:
            spot += ((offset >> bit) & 1) << (bits - 1 - bit)
        place.append(spot)
    return np.array(place, np.int32)


def joined_kernel(near_ref, far_ref, out_ref):
    half = near_ref.shape[0]
    out_ref[:half] = near_ref[...]
    out_ref[half:] = far_ref[...]


def gather_lists(own, beside):
    lists, order = own, [0]
    for bit in reversed(range(lax.axis_size("rows").bit_length() - 1)):
        arrived = swap(lists, 1 << bit)
        out = jax.ShapeDtypeStruct((2 * lists.shape[0], lists.shape[1]), lists.dtype)
        lists = call(joined_kernel, out, lists, arrived, name="joined")
        if len(order) == 1:
            found = beside(lists)
        order = order + [offset | 1 << bit for offset in order]
    return lists, np.argsort(np.array(order)).astype(np.int32), found


def gather_orders(count):
    low, shift, wide = stages(count)
    x = 1 << low[-1]
    early = [[0, x], [1 << shift, 1 << shift | x], [2 << shift, 3 << shift]]
    late = [[2 << shift | x, 3 << shift | x]]
    for bit in reversed(low[:-1]):
        early = early + [[offset | 1 << bit for offset in offsets] for offsets in early]
        late = late + [[offset | 1 << bit for offset in offsets] for offsets in late]
    return early, late


def gather_panels(panel, near, tokens, forward):
    low, shift, wide = stages(lax.axis_size("rows"))
    x = 1 << low[-1]
    fars = [swap(panel, 2 << shift), swap(panel, 3 << shift)]
    pair = stacked([panel, near], tokens[0])
    early = [pair, swap(pair, 1 << shift), stacked(fars, tokens[1])]
    late = swap(early[2], x)
    for bit in reversed(low[:-1]):
        early = early + [swap(array, 1 << bit) for array in early]
    count = 2 * len(early)
    out = forward(early, 0, None)
    late = [stacked([late[0], late[1]], out)]
    for bit in reversed(low[:-1]):
        late = late + [swap(array, 1 << bit) for array in late]
    return forward(late, count, out)


def reduce_panels(kept, sent):
    low, shift, wide = stages(lax.axis_size("rows"))
    x = 1 << low[-1]
    for bit in low[:-2]:
        arrived = swap(sent, 1 << bit)
        half = kept.shape[0] // 2
        sent = (kept[half:] + arrived[half:]).astype(jnp.bfloat16)
        kept = kept[:half] + arrived[:half]
    arrived = swap(sent, 1 << low[-2])
    kept, over_x, over_z = added(kept, arrived)
    return kept, swap(over_x, x), swap(over_z, 1 << shift)


def finish_panels(kept, over_x, over_z):
    low, shift, wide = stages(lax.axis_size("rows"))
    x = 1 << low[-1]
    terms = [swap((kept[2 + far] + over_x[far]).astype(jnp.bfloat16), (2 + far) << shift) for far in (1, 0)]
    return [kept[0], over_z[0], swap((kept[1] + over_z[1]).astype(jnp.bfloat16), x)] + terms


def added_kernel(kept_ref, arrived_ref, out_ref, over_x_ref, over_z_ref):
    def total(place):
        return kept_ref[place] + arrived_ref[place].astype(jnp.float32)

    for index, place in enumerate((0, 4, 2, 3)):
        out_ref[index] = total(place)
    for index, place in enumerate((6, 7)):
        over_x_ref[index] = total(place).astype(jnp.bfloat16)
    for index, place in enumerate((1, 5)):
        over_z_ref[index] = total(place).astype(jnp.bfloat16)


def added(kept, arrived):
    shape = jax.ShapeDtypeStruct
    half = shape((2, *kept.shape[1:]), jnp.bfloat16)
    return call(added_kernel, (shape((4, *kept.shape[1:]), jnp.float32), half, half), kept, arrived, name="added")


def stacked_kernel(*refs):
    for index, ref in enumerate(refs[:-2]):
        refs[-1][index] = ref[...]


def stacked(pieces, token):
    out = jax.ShapeDtypeStruct((len(pieces), *pieces[0].shape), pieces[0].dtype)
    return call(stacked_kernel, out, *pieces, token, name="stacked", specs=[VMEM] * len(pieces) + [ANY])


def reduce_small(array):
    low, shift, wide = stages(lax.axis_size("rows"))
    for bit in low:
        array = array + swap(array, 1 << bit)
    others = [swap(array, far << shift) for far in range(1, wide)]
    total = array + others[0]
    if wide == 4:
        total = total + (others[1] + others[2])
    return total


def tile_place(tile, fixed_ref, list_ref, sizes):
    count, capacity, tiles, tile_size = sizes
    me = fixed_ref[0]
    slot = fixed_ref[1 + 2 * count + tiles + tile]
    offset = (slot // capacity) ^ me
    block = list_ref[fixed_ref[1 + count + offset], me * capacity + slot % capacity]
    row = fixed_ref[1 + 2 * count + tile]
    own = pl.ds(pl.multiple_of(row * tile_size, tile_size), tile_size)
    other = pl.ds(pl.multiple_of(block * tile_size, tile_size), tile_size)
    return own, fixed_ref[1 + offset], other


def backward_product(tile, row, high_ref, low_ref, tiles_ref):
    tile_size = tiles_ref.shape[1]
    width = high_ref.shape[0]
    own = pl.ds(pl.multiple_of(row * tile_size, tile_size), tile_size)
    left = jnp.concatenate([high_ref[:, own], low_ref[:, own]], axis=0)
    both = jnp.dot(left, tiles_ref[tile], preferred_element_type=jnp.float32)
    return both[:width] + both[width:]


def over_tiles(tiles, body):
    def some(step, carry):
        for u in range(UNROLL):
            body(step * UNROLL + u)
        return carry

    lax.fori_loop(0, tiles // UNROLL, some, 0)


def products_kernel(rows_ref, start_ref, tiles_ref, token_ref, out_ref, held_ref, high_ref, low_ref, panel, arrived):
    tiles = out_ref.shape[0]
    whole = pltpu.make_async_copy(start_ref, panel, arrived.at[tiles // UNROLL])

    def copy(chunk):
        some = pl.ds(chunk * UNROLL, UNROLL)
        return pltpu.make_async_copy(tiles_ref.at[some], held_ref.at[some], arrived.at[chunk])

    whole.start()
    for chunk in range(tiles // UNROLL):
        copy(chunk).start()
    whole.wait()
    split_kernel(panel, high_ref, low_ref)
    for chunk in range(tiles // UNROLL):
        copy(chunk).wait()
        for tile in range(chunk * UNROLL, (chunk + 1) * UNROLL):
            out_ref[tile] = backward_product(tile, rows_ref[tile], high_ref, low_ref, held_ref)


def sums_kernel(fixed_ref, list_ref, products_ref, token_ref, kept_ref, sent_ref, total, *, sizes):
    half = kept_ref.shape[0]
    total[...] = jnp.zeros_like(total)

    def one(tile):
        own, piece, other = tile_place(tile, fixed_ref, list_ref, sizes)
        total[piece, :, other] += products_ref[tile].astype(total.dtype)

    over_tiles(sizes[2], one)
    kept_ref[...] = total[:half].astype(kept_ref.dtype)
    sent_ref[...] = total[half:].astype(sent_ref.dtype)


def backward_kernel(fixed_ref, list_ref, high_ref, low_ref, tiles_ref, kept_ref, sent_ref, total, *, sizes):
    count, _, tiles, _ = sizes
    half = kept_ref.shape[0]
    total[...] = jnp.zeros_like(total)

    def one(tile):
        own, piece, other = tile_place(tile, fixed_ref, list_ref, sizes)
        found = backward_product(tile, fixed_ref[1 + 2 * count + tile], high_ref, low_ref, tiles_ref)
        total[piece, :, other] += found.astype(total.dtype)

    over_tiles(tiles, one)
    kept_ref[...] = total[:half].astype(kept_ref.dtype)
    sent_ref[...] = total[half:].astype(sent_ref.dtype)


def plan_kernel(fixed_ref, list_ref, plan_ref, *, sizes, early):
    count, capacity, tiles, _ = sizes
    me = fixed_ref[0]

    def one(tile, found):
        front, back = found
        slot = fixed_ref[1 + 2 * count + tiles + tile]
        offset = (slot // capacity) ^ me
        block = list_ref[fixed_ref[1 + count + offset], me * capacity + slot % capacity]
        piece = fixed_ref[1 + 2 * count + 2 * tiles + offset]
        first = piece < early
        place = jnp.where(first, front, back)
        plan_ref[place] = ((tile * 256 + piece) * 16 + fixed_ref[1 + 2 * count + tile]) * 16 + block
        more = first.astype(jnp.int32)
        return front + more, back - (1 - more)

    front, _ = lax.fori_loop(0, tiles, one, (0, tiles - 1))
    plan_ref[tiles] = front


def forward_kernel(plan_ref, tiles_ref, *refs, groups, base, late):
    group_refs, (out_ref, pieces) = refs[:groups], refs[-2:]
    tiles, tile_size, _ = tiles_ref.shape
    for group, ref in enumerate(group_refs):
        pieces[group * 2 : (group + 1) * 2] = ref[...]
    out_ref[...] = refs[groups][...] if late else jnp.zeros_like(out_ref)
    front = plan_ref[tiles]
    start, end = (front, tiles) if late else (0, front)

    def some(step, carry):
        for u in range(8):
            at = start + step * 8 + u
            packed = plan_ref[jnp.minimum(at, tiles - 1)]
            block, row, piece, tile = packed % 16, packed // 16 % 16, packed // 256 % 256, packed // 65536
            piece = jnp.clip(piece - base, 0, groups * 2 - 1)
            own = pl.ds(pl.multiple_of(row * tile_size, tile_size), tile_size)
            other = pl.ds(pl.multiple_of(block * tile_size, tile_size), tile_size)
            found = lax.dot_general(
                pieces[piece, :, other], tiles_ref[tile], (((1,), (1,)), ((), ())), preferred_element_type=jnp.float32
            )
            out_ref[:, own] += jnp.where(at < end, found, 0.0)
        return carry

    lax.fori_loop(0, (end - start + 7) // 8, some, 0)


def split_kernel(whole_ref, high_ref, low_ref):
    high = whole_ref[...].astype(jnp.bfloat16)
    high_ref[...] = high
    low_ref[...] = (whole_ref[...] - high.astype(jnp.float32)).astype(jnp.bfloat16)


def combine_kernel(links_ref, panel_ref, forward_ref, *refs):
    term_refs, (out_ref, high_ref, low_ref) = refs[:-3], refs[-3:]
    out = (links_ref[...] - 1.0) * panel_ref[...] + forward_ref[...]
    for ref in term_refs:
        out = out + ref[...].astype(jnp.float32)
    out_ref[...] = out
    high = out.astype(jnp.bfloat16)
    high_ref[...] = high
    low_ref[...] = (out - high.astype(jnp.float32)).astype(jnp.bfloat16)


def factor_of(gram):
    width = gram.shape[0]
    lanes = -(-width // 128) * 128
    rows = lax.broadcasted_iota(jnp.int32, (width, lanes), 0)
    columns = lax.broadcasted_iota(jnp.int32, (width, lanes), 1)
    left = jnp.concatenate([gram, jnp.zeros((width, lanes - width), jnp.float32)], axis=1)
    right = (rows == columns).astype(jnp.float32)
    upper, inverse = [], []
    for at in range(0, width, STEP):
        spread = [jnp.broadcast_to(left[:, at + i : at + i + 1], left.shape) for i in range(STEP)]
        lefts, rights, factors = [], [], []
        for i in range(STEP):
            row, other, column = left[i : i + 1], right[i : i + 1], spread[i]
            for k in range(i):
                part = factors[k][i : i + 1]
                row = row - part * lefts[k]
                other = other - part * rights[k]
                column = column - part * factors[k]
            scale = lax.rsqrt(column[i : i + 1])
            lefts.append(row * scale)
            rights.append(other * scale)
            factors.append(column * scale)
        upper += lefts
        inverse += rights
        left, right = left[STEP:], right[STEP:]
        if at + STEP < width:
            for i in range(STEP):
                factor = factors[i][STEP:]
                left = left - factor * lefts[i]
                right = right - factor * rights[i]
    upper = jnp.concatenate(upper, axis=0)[:, :width]
    inverse = jnp.concatenate(inverse, axis=0)[:, :width]
    return jnp.where(rows[:, :width] >= columns[:, :width], upper.T, 0.0), inverse


def gram_kernel(links_ref, start_ref, first_ref, forward_ref, *refs):
    term_refs, (panels_ref, gram_ref) = refs[:-2], refs[-2:]
    width = start_ref.shape[0]
    second = links_ref[...] * first_ref[...] + forward_ref[...]
    for ref in term_refs:
        second = second + ref[...].astype(jnp.float32)
    panels_ref[:width] = start_ref[...]
    panels_ref[width : 2 * width] = first_ref[...]
    panels_ref[2 * width :] = second
    gram_ref[...] = product_t(panels_ref[...], panels_ref[...])


def last_kernel(gram_ref, panels_ref, out_ref, couplings_ref, factors_ref, *, scale):
    width = out_ref.shape[0]
    factor, inverse = factor_of(gram_ref[...])
    out_ref[...] = product(inverse[2 * width :] * scale, panels_ref[...])

    def block(of, row, column):
        return of[row * width : (row + 1) * width, column * width : (column + 1) * width]

    rows = lax.broadcasted_iota(jnp.int32, (width, width), 0)
    columns = lax.broadcasted_iota(jnp.int32, (width, width), 1)
    unit = (rows == columns).astype(jnp.float32)
    couplings_ref[0] = product(block(inverse, 0, 0), block(factor, 1, 0)).T + unit
    turned = product(block(inverse, 1, 0), block(factor, 1, 1)) + product(block(inverse, 1, 1), block(factor, 2, 1))
    couplings_ref[1] = turned.T
    factors_ref[0] = jnp.where(rows >= columns, product(block(inverse, 0, 0), block(factor, 1, 1)), 0.0)
    factors_ref[1] = jnp.where(rows >= columns, product(block(inverse, 1, 1), block(factor, 2, 2)), 0.0)


def room_for(*arrays):
    return (2 << 20) + sum(math.prod(array.shape) * jnp.dtype(array.dtype).itemsize for array in arrays)


def call(kernel, out, *args, name, scratch=(), specs=None, cost=None):
    return pl.pallas_call(
        kernel,
        out_shape=out,
        in_specs=specs or [VMEM] * len(args),
        out_specs=jax.tree.map(lambda _: VMEM, out),
        scratch_shapes=list(scratch),
        compiler_params=pltpu.CompilerParams(vmem_limit_bytes=room_for(*args, *jax.tree.leaves(out), *scratch)),
        cost_estimate=cost,
        name=name,
    )(*args)


def on_device(tile_values, tile_rows, tile_slots, send_list, self_links, start_panel):
    count = lax.axis_size("rows")
    width, here = start_panel.shape
    tiles, tile_size, _ = tile_values.shape
    capacity = send_list.shape[2]
    f32, bf16 = jnp.float32, jnp.bfloat16
    shape = jax.ShapeDtypeStruct
    links = self_links[None, :]
    me = lax.axis_index("rows").astype(jnp.int32).reshape(1)
    panel = shape((width, here), f32)
    half = shape((width, here), bf16)
    cost = pl.CostEstimate(flops=2 * tiles * width * tile_size * tile_size, bytes_accessed=1 << 10, transcendentals=0)

    def first_products(token):
        return pl.pallas_call(
            products_kernel,
            out_shape=(shape((tiles, width, tile_size), f32), pltpu.VMEM(tile_values.shape, bf16), half, half),
            in_specs=[SMEM, ANY, ANY, ANY],
            out_specs=(VMEM,) * 4,
            scratch_shapes=[pltpu.VMEM((width, here), f32), pltpu.SemaphoreType.DMA((tiles // UNROLL + 1,))],
            compiler_params=pltpu.CompilerParams(vmem_limit_bytes=room_for(tile_values, panel, panel, shape((tiles, width, tile_size), f32))),
            cost_estimate=cost,
            name="products",
        )(
            tile_rows, pltpu.with_memory_space_constraint(start_panel, pltpu.HBM),
            pltpu.with_memory_space_constraint(tile_values, pltpu.HBM), token,
        )

    lists, list_place, (products, held, high, low) = gather_lists(send_list.reshape(1, -1), first_products)
    orders = gather_orders(count)
    order = [offset for group in orders for offsets in group for offset in offsets]
    gathered_place = np.argsort(np.array(order)).astype(np.int32)
    early_pieces = 2 * len(orders[0])
    fixed = jnp.concatenate(
        [me, jnp.asarray(positions(count)), jnp.asarray(list_place), tile_rows, tile_slots, jnp.asarray(gathered_place)]
    )
    indices = (fixed, lists)
    sizes = (count, capacity, tiles, tile_size)
    spec = [SMEM] * len(indices)
    total_type = f32 if count <= 16 else bf16

    sums = (shape((count // 2, width, here), total_type), shape((count // 2, width, here), bf16))
    scratch = [pltpu.VMEM((count, width, here), total_type)]

    def first_sums(token):
        return call(
            functools.partial(sums_kernel, sizes=sizes), sums, *indices, products, token,
            name="sums", specs=spec + [VMEM, ANY], scratch=scratch, cost=cost,
        )

    def backward(high, low, token):
        return call(
            functools.partial(backward_kernel, sizes=sizes), sums, *indices, high, low, held,
            name="backward", specs=spec + [VMEM] * 3, scratch=scratch, cost=cost,
        )

    plan = pl.pallas_call(
        functools.partial(plan_kernel, sizes=sizes, early=early_pieces),
        out_shape=shape((tiles + 1,), jnp.int32), in_specs=spec, out_specs=SMEM, name="plan",
        compiler_params=pltpu.CompilerParams(vmem_limit_bytes=1 << 20),
    )(*indices)

    def forward(groups, base, before):
        late = before is not None
        return call(
            functools.partial(forward_kernel, groups=len(groups), base=base, late=late),
            shape((width, here), f32),
            plan, held, *groups, *([before] if late else []),
            name="late" if late else "early", specs=[SMEM] + [VMEM] * (1 + len(groups) + late),
            scratch=[pltpu.VMEM((2 * len(groups), width, here), bf16)], cost=cost,
        )

    def applied(high, sums):
        near = swap(high, 1 << stages(count)[0][-1])
        kept, over_x, over_z = reduce_panels(*sums(high))
        terms = finish_panels(kept, over_x, over_z)
        return [gather_panels(high, near, (kept, over_x), forward)] + terms

    terms = applied(high, first_sums)
    first, high, low = call(combine_kernel, (panel, half, half), links, start_panel, *terms, name="combine")
    terms = applied(high, functools.partial(backward, high, low))
    all_panels = (ITERS + 1) * width
    panels, gram = call(
        gram_kernel, (shape((all_panels, here), f32), shape((all_panels, all_panels), f32)), links, start_panel, first, *terms, name="gram"
    )
    both = shape((ITERS, width, width), f32)
    return call(
        functools.partial(last_kernel, scale=math.sqrt(here * count)), (panel, both, both), reduce_small(gram), panels, name="last"
    )


def solution(mesh):
    placed = (
        P(("groups", "rows"), None, None),
        P(("groups", "rows")),
        P(("groups", "rows")),
        P(("groups", "rows"), None, None),
        P(("groups", "rows")),
        P(None, ("groups", "rows")),
    )
    return jax.shard_map(
        on_device,
        mesh=mesh,
        in_specs=placed,
        out_specs=(P(None, ("groups", "rows")), P("groups", None, None), P("groups", None, None)),
        check_vma=False,
    )
```

```python
import functools
import math

import jax
import jax.numpy as jnp
import numpy as np
from jax import lax
from jax.experimental import pallas as pl
from jax.experimental.pallas import tpu as pltpu
from jax.sharding import PartitionSpec as P

precise = lax.Precision.HIGHEST
SMEM = pl.BlockSpec(memory_space=pltpu.SMEM)
VMEM = pl.BlockSpec(memory_space=pltpu.VMEM)
ANY = pl.BlockSpec(memory_space=pl.ANY)
UNROLL = 16
STEP = 16
ITERS = 2


def product(left, right):
    return lax.dot_general(left, right, (((1,), (0,)), ((), ())), precision=precise, preferred_element_type=jnp.float32)


def product_t(left, right):
    return lax.dot_general(left, right, (((1,), (1,)), ((), ())), precision=precise, preferred_element_type=jnp.float32)


def t_product(left, right):
    return lax.dot_general(left, right, (((0,), (0,)), ((), ())), precision=precise, preferred_element_type=jnp.float32)


def swap(array, offset):
    count = lax.axis_size("rows")
    return lax.ppermute(array, "rows", [(place, place ^ offset) for place in range(count)])


def stages(count):
    bits = count.bit_length() - 1
    top = min(2, bits)
    return list(range(bits - top)), bits - top, 1 << top


def positions(count):
    low, shift, wide = stages(count)
    bits = count.bit_length() - 1
    place = []
    for offset in range(count):
        spot = offset >> shift
        for bit in low:
            spot += ((offset >> bit) & 1) << (bits - 1 - bit)
        place.append(spot)
    return np.array(place, np.int32)


def joined_kernel(near_ref, far_ref, out_ref):
    half = near_ref.shape[0]
    out_ref[:half] = near_ref[...]
    out_ref[half:] = far_ref[...]


def gather_lists(own, beside):
    lists, order = own, [0]
    for bit in reversed(range(lax.axis_size("rows").bit_length() - 1)):
        arrived = swap(lists, 1 << bit)
        out = jax.ShapeDtypeStruct((2 * lists.shape[0], lists.shape[1]), lists.dtype)
        lists = call(joined_kernel, out, lists, arrived, name="joined")
        if len(order) == 1:
            found = beside(lists)
        order = order + [offset | 1 << bit for offset in order]
    return lists, np.argsort(np.array(order)).astype(np.int32), found


def gather_orders(count):
    low, shift, wide = stages(count)
    x = 1 << low[-1]
    early = [[0, x], [2 << shift, 3 << shift]]
    late = [[1 << shift, 1 << shift | x], [2 << shift | x, 3 << shift | x]]
    for bit in reversed(low[:-1]):
        early = early + [[offset | 1 << bit for offset in offsets] for offsets in early]
        late = late + [[offset | 1 << bit for offset in offsets] for offsets in late]
    return early, late


def gather_panels(panel, near, tokens, forward):
    low, shift, wide = stages(lax.axis_size("rows"))
    x = 1 << low[-1]
    fars = [swap(panel, 2 << shift), swap(panel, 3 << shift)]
    pair = stacked([panel, near], tokens[0])
    early = [pair, stacked(fars, tokens[1])]
    beside = swap(pair, 1 << shift)
    late = swap(early[1], x)
    for bit in reversed(low[:-1]):
        early = early + [swap(array, 1 << bit) for array in early]
    count = 2 * len(early)
    out = forward(early, 0, None)
    late = [stacked([beside[0], beside[1]], out), stacked([late[0], late[1]], out)]
    for bit in reversed(low[:-1]):
        late = late + [swap(array, 1 << bit) for array in late]
    return forward(late, count, out)


def reduce_panels(kept, sent):
    low, shift, wide = stages(lax.axis_size("rows"))
    x = 1 << low[-1]
    for bit in low[:-2]:
        arrived = swap(sent, 1 << bit)
        half = kept.shape[0] // 2
        sent = (kept[half:] + arrived[half:]).astype(jnp.bfloat16)
        kept = kept[:half] + arrived[:half]
    arrived = swap(sent, 1 << low[-2])
    kept, over_x, over_z = added(kept, arrived)
    return kept, swap(over_x, x), swap(over_z, 1 << shift)


def finish_panels(kept, over_x, over_z):
    low, shift, wide = stages(lax.axis_size("rows"))
    x = 1 << low[-1]
    terms = [swap((kept[2 + far] + over_x[far]).astype(jnp.bfloat16), (2 + far) << shift) for far in (1, 0)]
    return [kept[0], over_z[0], swap((kept[1] + over_z[1]).astype(jnp.bfloat16), x)] + terms


def added_kernel(kept_ref, arrived_ref, out_ref, over_x_ref, over_z_ref):
    def total(place):
        return kept_ref[place] + arrived_ref[place].astype(jnp.float32)

    for index, place in enumerate((0, 4, 2, 3)):
        out_ref[index] = total(place)
    for index, place in enumerate((6, 7)):
        over_x_ref[index] = total(place).astype(jnp.bfloat16)
    for index, place in enumerate((1, 5)):
        over_z_ref[index] = total(place).astype(jnp.bfloat16)


def added(kept, arrived):
    shape = jax.ShapeDtypeStruct
    half = shape((2, *kept.shape[1:]), jnp.bfloat16)
    return call(added_kernel, (shape((4, *kept.shape[1:]), jnp.float32), half, half), kept, arrived, name="added")


def stacked_kernel(*refs):
    for index, ref in enumerate(refs[:-2]):
        refs[-1][index] = ref[...]


def stacked(pieces, token):
    out = jax.ShapeDtypeStruct((len(pieces), *pieces[0].shape), pieces[0].dtype)
    return call(stacked_kernel, out, *pieces, token, name="stacked", specs=[VMEM] * len(pieces) + [ANY])


def reduce_small(array):
    low, shift, wide = stages(lax.axis_size("rows"))
    for bit in low:
        array = array + swap(array, 1 << bit)
    others = [swap(array, far << shift) for far in range(1, wide)]
    total = array + others[0]
    if wide == 4:
        total = total + (others[1] + others[2])
    return total


def parted(number, size):
    if size & (size - 1):
        return number // size, number % size
    return lax.shift_right_logical(number, size.bit_length() - 1), number & (size - 1)


def tile_place(tile, fixed_ref, list_ref, sizes):
    count, capacity, tiles, tile_size = sizes
    me = fixed_ref[0]
    slot = fixed_ref[1 + 2 * count + tiles + tile]
    sender, within = parted(slot, capacity)
    offset = sender ^ me
    block = list_ref[fixed_ref[1 + count + offset], me * capacity + within]
    row = fixed_ref[1 + 2 * count + tile]
    own = pl.ds(pl.multiple_of(row * tile_size, tile_size), tile_size)
    other = pl.ds(pl.multiple_of(block * tile_size, tile_size), tile_size)
    return own, fixed_ref[1 + offset], other


def backward_product(tile, row, high_ref, low_ref, tiles_ref):
    tile_size = tiles_ref.shape[1]
    width = high_ref.shape[0]
    own = pl.ds(pl.multiple_of(row * tile_size, tile_size), tile_size)
    left = jnp.concatenate([high_ref[:, own], low_ref[:, own]], axis=0)
    both = jnp.dot(left, tiles_ref[tile], preferred_element_type=jnp.float32)
    return both[:width] + both[width:]


def over_tiles(tiles, body):
    def some(step, carry):
        for u in range(UNROLL):
            body(step * UNROLL + u)
        return carry

    lax.fori_loop(0, tiles // UNROLL, some, 0)


def products_kernel(rows_ref, start_ref, tiles_ref, token_ref, out_ref, held_ref, high_ref, low_ref, panel, arrived):
    tiles = out_ref.shape[0]
    whole = pltpu.make_async_copy(start_ref, panel, arrived.at[tiles // UNROLL])

    def copy(chunk):
        some = pl.ds(chunk * UNROLL, UNROLL)
        return pltpu.make_async_copy(tiles_ref.at[some], held_ref.at[some], arrived.at[chunk])

    whole.start()
    for chunk in range(tiles // UNROLL):
        copy(chunk).start()
    whole.wait()
    split_kernel(panel, high_ref, low_ref)
    for chunk in range(tiles // UNROLL):
        copy(chunk).wait()
        for tile in range(chunk * UNROLL, (chunk + 1) * UNROLL):
            out_ref[tile] = backward_product(tile, rows_ref[tile], high_ref, low_ref, held_ref)


def sums_kernel(fixed_ref, list_ref, products_ref, token_ref, kept_ref, sent_ref, total, *, sizes):
    half = kept_ref.shape[0]
    total[...] = jnp.zeros_like(total)

    def one(tile):
        own, piece, other = tile_place(tile, fixed_ref, list_ref, sizes)
        total[piece, :, other] += products_ref[tile].astype(total.dtype)

    over_tiles(sizes[2], one)
    kept_ref[...] = total[:half].astype(kept_ref.dtype)
    sent_ref[...] = total[half:].astype(sent_ref.dtype)


def backward_kernel(fixed_ref, list_ref, high_ref, low_ref, tiles_ref, kept_ref, sent_ref, total, *, sizes):
    count, _, tiles, _ = sizes
    half = kept_ref.shape[0]
    total[...] = jnp.zeros_like(total)

    def one(tile):
        own, piece, other = tile_place(tile, fixed_ref, list_ref, sizes)
        found = backward_product(tile, fixed_ref[1 + 2 * count + tile], high_ref, low_ref, tiles_ref)
        total[piece, :, other] += found.astype(total.dtype)

    over_tiles(tiles, one)
    kept_ref[...] = total[:half].astype(kept_ref.dtype)
    sent_ref[...] = total[half:].astype(sent_ref.dtype)


def plan_kernel(fixed_ref, list_ref, plan_ref, *, sizes, early):
    count, capacity, tiles, _ = sizes
    me = fixed_ref[0]

    def one(tile, found):
        front, back = found
        slot = fixed_ref[1 + 2 * count + tiles + tile]
        sender, within = parted(slot, capacity)
        offset = sender ^ me
        block = list_ref[fixed_ref[1 + count + offset], me * capacity + within]
        piece = fixed_ref[1 + 2 * count + 2 * tiles + offset]
        first = piece < early
        place = jnp.where(first, front, back)
        plan_ref[place] = ((tile * 256 + piece) * 16 + fixed_ref[1 + 2 * count + tile]) * 16 + block
        more = first.astype(jnp.int32)
        return front + more, back - (1 - more)

    front, _ = lax.fori_loop(0, tiles, one, (0, tiles - 1))
    plan_ref[tiles] = front


def forward_kernel(plan_ref, tiles_ref, *refs, groups, base, late):
    group_refs, (out_ref, pieces) = refs[:groups], refs[-2:]
    tiles, tile_size, _ = tiles_ref.shape
    for group, ref in enumerate(group_refs):
        pieces[group * 2 : (group + 1) * 2] = ref[...]
    out_ref[...] = refs[groups][...] if late else jnp.zeros_like(out_ref)
    front = plan_ref[tiles]
    start, end = (front, tiles) if late else (0, front)

    def some(step, carry):
        for u in range(8):
            at = start + step * 8 + u
            packed = plan_ref[jnp.minimum(at, tiles - 1)]
            rest, block = parted(packed, 16)
            rest, row = parted(rest, 16)
            tile, piece = parted(rest, 256)
            piece = jnp.clip(piece - base, 0, groups * 2 - 1)
            own = pl.ds(pl.multiple_of(row * tile_size, tile_size), tile_size)
            other = pl.ds(pl.multiple_of(block * tile_size, tile_size), tile_size)
            found = lax.dot_general(
                pieces[piece, :, other], tiles_ref[tile], (((1,), (1,)), ((), ())), preferred_element_type=jnp.float32
            )
            out_ref[:, own] += jnp.where(at < end, found, 0.0)
        return carry

    lax.fori_loop(0, (end - start + 7) // 8, some, 0)


def split_kernel(whole_ref, high_ref, low_ref):
    high = whole_ref[...].astype(jnp.bfloat16)
    high_ref[...] = high
    low_ref[...] = (whole_ref[...] - high.astype(jnp.float32)).astype(jnp.bfloat16)


def combine_kernel(links_ref, panel_ref, forward_ref, *refs):
    term_refs, (out_ref, high_ref, low_ref) = refs[:-3], refs[-3:]
    out = (links_ref[...] - 1.0) * panel_ref[...] + forward_ref[...]
    for ref in term_refs:
        out = out + ref[...].astype(jnp.float32)
    out_ref[...] = out
    high = out.astype(jnp.bfloat16)
    high_ref[...] = high
    low_ref[...] = (out - high.astype(jnp.float32)).astype(jnp.bfloat16)


def factor_of(gram):
    width = gram.shape[0]
    lanes = -(-width // 128) * 128
    rows = lax.broadcasted_iota(jnp.int32, (width, lanes), 0)
    columns = lax.broadcasted_iota(jnp.int32, (width, lanes), 1)
    left = jnp.concatenate([gram, jnp.zeros((width, lanes - width), jnp.float32)], axis=1)
    right = (rows == columns).astype(jnp.float32)
    upper, inverse = [], []
    for at in range(0, width, STEP):
        spread = [jnp.broadcast_to(left[:, at + i : at + i + 1], left.shape) for i in range(STEP)]
        lefts, rights, factors = [], [], []
        for i in range(STEP):
            row, other, column = left[i : i + 1], right[i : i + 1], spread[i]
            for k in range(i):
                part = factors[k][i : i + 1]
                row = row - part * lefts[k]
                other = other - part * rights[k]
                column = column - part * factors[k]
            scale = lax.rsqrt(column[i : i + 1])
            lefts.append(row * scale)
            rights.append(other * scale)
            factors.append(column * scale)
        upper += lefts
        inverse += rights
        left, right = left[STEP:], right[STEP:]
        if at + STEP < width:
            for i in range(STEP):
                factor = factors[i][STEP:]
                left = left - factor * lefts[i]
                right = right - factor * rights[i]
    upper = jnp.concatenate(upper, axis=0)[:, :width]
    inverse = jnp.concatenate(inverse, axis=0)[:, :width]
    return jnp.where(rows[:, :width] >= columns[:, :width], upper.T, 0.0), inverse


def gram_kernel(links_ref, start_ref, first_ref, forward_ref, *refs):
    term_refs, (panels_ref, gram_ref) = refs[:-2], refs[-2:]
    width = start_ref.shape[0]
    second = links_ref[...] * first_ref[...] + forward_ref[...]
    for ref in term_refs:
        second = second + ref[...].astype(jnp.float32)
    panels_ref[:width] = start_ref[...]
    panels_ref[width : 2 * width] = first_ref[...]
    panels_ref[2 * width :] = second
    gram = product_t(panels_ref[...], panels_ref[...])

    def block(row, column):
        return gram[row * width : (row + 1) * width, column * width : (column + 1) * width]

    gram_ref[:width] = jnp.concatenate([block(0, 0), block(1, 0), block(1, 1), block(2, 0)], axis=1)
    half = width // 2
    others = [part for of in (block(2, 1), block(2, 2)) for part in (of[:half], of[half:])]
    gram_ref[width:] = jnp.concatenate(others, axis=1)


def last_kernel(gram_ref, panels_ref, out_ref, couplings_ref, factors_ref, *, scale):
    width = out_ref.shape[0]
    def sent(place):
        return gram_ref[:width, place * width : (place + 1) * width]

    def halves(place):
        return jnp.concatenate([gram_ref[width:, at * width : (at + 1) * width] for at in (place, place + 1)], axis=0)

    gram = jnp.concatenate(
        [
            jnp.concatenate([sent(0), sent(1).T, sent(3).T], axis=1),
            jnp.concatenate([sent(1), sent(2), halves(0).T], axis=1),
            jnp.concatenate([sent(3), halves(0), halves(2)], axis=1),
        ],
        axis=0,
    )
    factor, inverse = factor_of(gram)
    out_ref[...] = product(inverse[2 * width :] * scale, panels_ref[...])

    def block(of, row, column):
        return of[row * width : (row + 1) * width, column * width : (column + 1) * width]

    rows = lax.broadcasted_iota(jnp.int32, (width, width), 0)
    columns = lax.broadcasted_iota(jnp.int32, (width, width), 1)
    unit = (rows == columns).astype(jnp.float32)
    couplings_ref[0] = product(block(inverse, 0, 0), block(factor, 1, 0)).T + unit
    turned = product(block(inverse, 1, 0), block(factor, 1, 1)) + product(block(inverse, 1, 1), block(factor, 2, 1))
    couplings_ref[1] = turned.T
    factors_ref[0] = jnp.where(rows >= columns, product(block(inverse, 0, 0), block(factor, 1, 1)), 0.0)
    factors_ref[1] = jnp.where(rows >= columns, product(block(inverse, 1, 1), block(factor, 2, 2)), 0.0)


def room_for(*arrays):
    return (2 << 20) + sum(math.prod(array.shape) * jnp.dtype(array.dtype).itemsize for array in arrays)


def call(kernel, out, *args, name, scratch=(), specs=None, cost=None):
    return pl.pallas_call(
        kernel,
        out_shape=out,
        in_specs=specs or [VMEM] * len(args),
        out_specs=jax.tree.map(lambda _: VMEM, out),
        scratch_shapes=list(scratch),
        compiler_params=pltpu.CompilerParams(vmem_limit_bytes=room_for(*args, *jax.tree.leaves(out), *scratch)),
        cost_estimate=cost,
        name=name,
    )(*args)


def on_device(tile_values, tile_rows, tile_slots, send_list, self_links, start_panel):
    count = lax.axis_size("rows")
    width, here = start_panel.shape
    tiles, tile_size, _ = tile_values.shape
    capacity = send_list.shape[2]
    f32, bf16 = jnp.float32, jnp.bfloat16
    shape = jax.ShapeDtypeStruct
    links = self_links[None, :]
    me = lax.axis_index("rows").astype(jnp.int32).reshape(1)
    panel = shape((width, here), f32)
    half = shape((width, here), bf16)
    cost = pl.CostEstimate(flops=2 * tiles * width * tile_size * tile_size, bytes_accessed=1 << 10, transcendentals=0)

    def first_products(token):
        return pl.pallas_call(
            products_kernel,
            out_shape=(shape((tiles, width, tile_size), f32), pltpu.VMEM(tile_values.shape, bf16), half, half),
            in_specs=[SMEM, ANY, ANY, ANY],
            out_specs=(VMEM,) * 4,
            scratch_shapes=[pltpu.VMEM((width, here), f32), pltpu.SemaphoreType.DMA((tiles // UNROLL + 1,))],
            compiler_params=pltpu.CompilerParams(vmem_limit_bytes=room_for(tile_values, panel, panel, shape((tiles, width, tile_size), f32))),
            cost_estimate=cost,
            name="products",
        )(
            tile_rows, pltpu.with_memory_space_constraint(start_panel, pltpu.HBM),
            pltpu.with_memory_space_constraint(tile_values, pltpu.HBM), token,
        )

    lists, list_place, (products, held, high, low) = gather_lists(send_list.reshape(1, -1), first_products)
    orders = gather_orders(count)
    order = [offset for group in orders for offsets in group for offset in offsets]
    gathered_place = np.argsort(np.array(order)).astype(np.int32)
    early_pieces = 2 * len(orders[0])
    fixed = jnp.concatenate(
        [me, jnp.asarray(positions(count)), jnp.asarray(list_place), tile_rows, tile_slots, jnp.asarray(gathered_place)]
    )
    indices = (fixed, lists)
    sizes = (count, capacity, tiles, tile_size)
    spec = [SMEM] * len(indices)
    total_type = f32 if count <= 16 else bf16

    sums = (shape((count // 2, width, here), total_type), shape((count // 2, width, here), bf16))
    scratch = [pltpu.VMEM((count, width, here), total_type)]

    def first_sums(token):
        return call(
            functools.partial(sums_kernel, sizes=sizes), sums, *indices, products, token,
            name="sums", specs=spec + [VMEM, ANY], scratch=scratch, cost=cost,
        )

    def backward(high, low, token):
        return call(
            functools.partial(backward_kernel, sizes=sizes), sums, *indices, high, low, held,
            name="backward", specs=spec + [VMEM] * 3, scratch=scratch, cost=cost,
        )

    plan = pl.pallas_call(
        functools.partial(plan_kernel, sizes=sizes, early=early_pieces),
        out_shape=shape((tiles + 1,), jnp.int32), in_specs=spec, out_specs=SMEM, name="plan",
        compiler_params=pltpu.CompilerParams(vmem_limit_bytes=1 << 20),
    )(*indices)

    def forward(groups, base, before):
        late = before is not None
        return call(
            functools.partial(forward_kernel, groups=len(groups), base=base, late=late),
            shape((width, here), f32),
            plan, held, *groups, *([before] if late else []),
            name="late" if late else "early", specs=[SMEM] + [VMEM] * (1 + len(groups) + late),
            scratch=[pltpu.VMEM((2 * len(groups), width, here), bf16)], cost=cost,
        )

    def applied(high, sums):
        near = swap(high, 1 << stages(count)[0][-1])
        kept, over_x, over_z = reduce_panels(*sums(high))
        terms = finish_panels(kept, over_x, over_z)
        return [gather_panels(high, near, (kept, kept), forward)] + terms

    terms = applied(high, first_sums)
    first, high, low = call(combine_kernel, (panel, half, half), links, start_panel, *terms, name="combine")
    terms = applied(high, functools.partial(backward, high, low))
    all_panels = (ITERS + 1) * width
    panels, gram = call(
        gram_kernel, (shape((all_panels, here), f32), shape((width + width // 2, 4 * width), f32)), links, start_panel, first, *terms, name="gram"
    )
    both = shape((ITERS, width, width), f32)
    return call(
        functools.partial(last_kernel, scale=math.sqrt(here * count)), (panel, both, both), reduce_small(gram), panels, name="last"
    )


def solution(mesh):
    placed = (
        P(("groups", "rows"), None, None),
        P(("groups", "rows")),
        P(("groups", "rows")),
        P(("groups", "rows"), None, None),
        P(("groups", "rows")),
        P(None, ("groups", "rows")),
    )
    return jax.shard_map(
        on_device,
        mesh=mesh,
        in_specs=placed,
        out_specs=(P(None, ("groups", "rows")), P("groups", None, None), P("groups", None, None)),
        check_vma=False,
    )
```

```python
import functools
import math

import jax
import jax.numpy as jnp
import numpy as np
from jax import lax
from jax.experimental import pallas as pl
from jax.experimental.pallas import tpu as pltpu
from jax.sharding import PartitionSpec as P

precise = lax.Precision.HIGHEST
SMEM = pl.BlockSpec(memory_space=pltpu.SMEM)
VMEM = pl.BlockSpec(memory_space=pltpu.VMEM)
ANY = pl.BlockSpec(memory_space=pl.ANY)
UNROLL = 16
STEP = 16
ITERS = 2


def product(left, right):
    return lax.dot_general(left, right, (((1,), (0,)), ((), ())), precision=precise, preferred_element_type=jnp.float32)


def product_t(left, right):
    return lax.dot_general(left, right, (((1,), (1,)), ((), ())), precision=precise, preferred_element_type=jnp.float32)


def t_product(left, right):
    return lax.dot_general(left, right, (((0,), (0,)), ((), ())), precision=precise, preferred_element_type=jnp.float32)


def swap(array, offset):
    count = lax.axis_size("rows")
    return lax.ppermute(array, "rows", [(place, place ^ offset) for place in range(count)])


def stages(count):
    bits = count.bit_length() - 1
    top = min(2, bits)
    return list(range(bits - top)), bits - top, 1 << top


def positions(count):
    low, shift, wide = stages(count)
    bits = count.bit_length() - 1
    place = []
    for offset in range(count):
        spot = offset >> shift
        for bit in low:
            spot += ((offset >> bit) & 1) << (bits - 1 - bit)
        place.append(spot)
    return np.array(place, np.int32)


def joined_kernel(near_ref, far_ref, out_ref):
    half = near_ref.shape[0]
    out_ref[:half] = near_ref[...]
    out_ref[half:] = far_ref[...]


def gather_lists(own, beside):
    lists, order = own, [0]
    for bit in reversed(range(lax.axis_size("rows").bit_length() - 1)):
        arrived = swap(lists, 1 << bit)
        out = jax.ShapeDtypeStruct((2 * lists.shape[0], lists.shape[1]), lists.dtype)
        lists = call(joined_kernel, out, lists, arrived, name="joined")
        if len(order) == 1:
            found = beside(lists)
        order = order + [offset | 1 << bit for offset in order]
    return lists, np.argsort(np.array(order)).astype(np.int32), found


def gather_orders(count):
    low, shift, wide = stages(count)
    x = 1 << low[-1]
    fars = [far << shift for far in range(1, wide)]
    early = [[0, x], fars]
    late = [[far | x for far in fars]]
    for bit in reversed(low[:-1]):
        early = early + [[offset | 1 << bit for offset in offsets] for offsets in early]
        late = late + [[offset | 1 << bit for offset in offsets] for offsets in late]
    return early, late


def gather_panels(panel, near, tokens, forward):
    low, shift, wide = stages(lax.axis_size("rows"))
    x = 1 << low[-1]
    fars = [swap(panel, far << shift) for far in range(1, wide)]
    early = [stacked([panel, near], tokens[0]), stacked(fars, tokens[1])]
    late = swap(early[1], x)
    for bit in reversed(low[:-1]):
        early = early + [swap(array, 1 << bit) for array in early]
    out = forward(early, 0, None)
    late = [whole(late, out)]
    for bit in reversed(low[:-1]):
        late = late + [swap(array, 1 << bit) for array in late]
    return forward(late, sum(array.shape[0] for array in early), out)


def reduce_panels(kept, sent):
    low, shift, wide = stages(lax.axis_size("rows"))
    x = 1 << low[-1]
    for bit in low[:-2]:
        arrived = swap(sent, 1 << bit)
        half = kept.shape[0] // 2
        sent = (kept[half:] + arrived[half:]).astype(jnp.bfloat16)
        kept = kept[:half] + arrived[:half]
    arrived = swap(sent, 1 << low[-2])
    kept, over_x, over_z = added(kept, arrived)
    return kept, swap(over_x, x), swap(over_z, 1 << shift)


def finish_panels(kept, over_x, over_z):
    low, shift, wide = stages(lax.axis_size("rows"))
    x = 1 << low[-1]
    terms = [swap((kept[2 + far] + over_x[far]).astype(jnp.bfloat16), (2 + far) << shift) for far in (1, 0)]
    return [kept[0], over_z[0], swap((kept[1] + over_z[1]).astype(jnp.bfloat16), x)] + terms


def added_kernel(kept_ref, arrived_ref, out_ref, over_x_ref, over_z_ref):
    def total(place):
        return kept_ref[place] + arrived_ref[place].astype(jnp.float32)

    for index, place in enumerate((0, 4, 2, 3)):
        out_ref[index] = total(place)
    for index, place in enumerate((6, 7)):
        over_x_ref[index] = total(place).astype(jnp.bfloat16)
    for index, place in enumerate((1, 5)):
        over_z_ref[index] = total(place).astype(jnp.bfloat16)


def added(kept, arrived):
    shape = jax.ShapeDtypeStruct
    half = shape((2, *kept.shape[1:]), jnp.bfloat16)
    return call(added_kernel, (shape((4, *kept.shape[1:]), jnp.float32), half, half), kept, arrived, name="added")


def whole_kernel(array_ref, token_ref, out_ref):
    out_ref[...] = array_ref[...]


def whole(array, token):
    out = jax.ShapeDtypeStruct(array.shape, array.dtype)
    return call(whole_kernel, out, array, token, name="whole", specs=[VMEM, ANY])


def stacked_kernel(*refs):
    for index, ref in enumerate(refs[:-2]):
        refs[-1][index] = ref[...]


def stacked(pieces, token):
    out = jax.ShapeDtypeStruct((len(pieces), *pieces[0].shape), pieces[0].dtype)
    return call(stacked_kernel, out, *pieces, token, name="stacked", specs=[VMEM] * len(pieces) + [ANY])


def reduce_small(array):
    low, shift, wide = stages(lax.axis_size("rows"))
    for bit in low:
        array = array + swap(array, 1 << bit)
    others = [swap(array, far << shift) for far in range(1, wide)]
    total = array + others[0]
    if wide == 4:
        total = total + (others[1] + others[2])
    return total


def parted(number, size):
    if size & (size - 1):
        return number // size, number % size
    return lax.shift_right_logical(number, size.bit_length() - 1), number & (size - 1)


def tile_place(tile, fixed_ref, list_ref, sizes):
    count, capacity, tiles, tile_size = sizes
    me = fixed_ref[0]
    slot = fixed_ref[1 + 2 * count + tiles + tile]
    sender, within = parted(slot, capacity)
    offset = sender ^ me
    block = list_ref[fixed_ref[1 + count + offset], me * capacity + within]
    row = fixed_ref[1 + 2 * count + tile]
    own = pl.ds(pl.multiple_of(row * tile_size, tile_size), tile_size)
    other = pl.ds(pl.multiple_of(block * tile_size, tile_size), tile_size)
    return own, fixed_ref[1 + offset], other


def backward_product(tile, row, high_ref, low_ref, tiles_ref):
    tile_size = tiles_ref.shape[1]
    width = high_ref.shape[0]
    own = pl.ds(pl.multiple_of(row * tile_size, tile_size), tile_size)
    left = jnp.concatenate([high_ref[:, own], low_ref[:, own]], axis=0)
    both = jnp.dot(left, tiles_ref[tile], preferred_element_type=jnp.float32)
    return both[:width] + both[width:]


def over_tiles(tiles, body):
    def some(step, carry):
        for u in range(UNROLL):
            body(step * UNROLL + u)
        return carry

    lax.fori_loop(0, tiles // UNROLL, some, 0)


def products_kernel(rows_ref, start_ref, tiles_ref, token_ref, out_ref, held_ref, high_ref, low_ref, panel, arrived):
    tiles = out_ref.shape[0]
    whole = pltpu.make_async_copy(start_ref, panel, arrived.at[tiles // UNROLL])

    def copy(chunk):
        some = pl.ds(chunk * UNROLL, UNROLL)
        return pltpu.make_async_copy(tiles_ref.at[some], held_ref.at[some], arrived.at[chunk])

    whole.start()
    for chunk in range(tiles // UNROLL):
        copy(chunk).start()
    whole.wait()
    split_kernel(panel, high_ref, low_ref)
    for chunk in range(tiles // UNROLL):
        copy(chunk).wait()
        for tile in range(chunk * UNROLL, (chunk + 1) * UNROLL):
            out_ref[tile] = backward_product(tile, rows_ref[tile], high_ref, low_ref, held_ref)


def sums_kernel(fixed_ref, list_ref, products_ref, token_ref, kept_ref, sent_ref, total, *, sizes):
    half = kept_ref.shape[0]
    total[...] = jnp.zeros_like(total)

    def one(tile):
        own, piece, other = tile_place(tile, fixed_ref, list_ref, sizes)
        total[piece, :, other] += products_ref[tile].astype(total.dtype)

    over_tiles(sizes[2], one)
    kept_ref[...] = total[:half].astype(kept_ref.dtype)
    sent_ref[...] = total[half:].astype(sent_ref.dtype)


def backward_kernel(fixed_ref, list_ref, high_ref, low_ref, tiles_ref, kept_ref, sent_ref, total, *, sizes):
    count, _, tiles, _ = sizes
    half = kept_ref.shape[0]
    total[...] = jnp.zeros_like(total)

    def one(tile):
        own, piece, other = tile_place(tile, fixed_ref, list_ref, sizes)
        found = backward_product(tile, fixed_ref[1 + 2 * count + tile], high_ref, low_ref, tiles_ref)
        total[piece, :, other] += found.astype(total.dtype)

    over_tiles(tiles, one)
    kept_ref[...] = total[:half].astype(kept_ref.dtype)
    sent_ref[...] = total[half:].astype(sent_ref.dtype)


def plan_kernel(fixed_ref, list_ref, plan_ref, *, sizes, early):
    count, capacity, tiles, _ = sizes
    me = fixed_ref[0]

    def one(tile, found):
        front, back = found
        slot = fixed_ref[1 + 2 * count + tiles + tile]
        sender, within = parted(slot, capacity)
        offset = sender ^ me
        block = list_ref[fixed_ref[1 + count + offset], me * capacity + within]
        piece = fixed_ref[1 + 2 * count + 2 * tiles + offset]
        first = piece < early
        place = jnp.where(first, front, back)
        plan_ref[place] = ((tile * 256 + piece) * 16 + fixed_ref[1 + 2 * count + tile]) * 16 + block
        more = first.astype(jnp.int32)
        return front + more, back - (1 - more)

    front, _ = lax.fori_loop(0, tiles, one, (0, tiles - 1))
    plan_ref[tiles] = front


def forward_kernel(plan_ref, tiles_ref, *refs, groups, base, late):
    group_refs, (out_ref, pieces) = refs[:groups], refs[-2:]
    tiles, tile_size, _ = tiles_ref.shape
    at = 0
    for ref in group_refs:
        pieces[at : at + ref.shape[0]] = ref[...]
        at += ref.shape[0]
    out_ref[...] = refs[groups][...] if late else jnp.zeros_like(out_ref)
    front = plan_ref[tiles]
    start, end = (front, tiles) if late else (0, front)

    def some(step, carry):
        for u in range(8):
            at = start + step * 8 + u
            packed = plan_ref[jnp.minimum(at, tiles - 1)]
            rest, block = parted(packed, 16)
            rest, row = parted(rest, 16)
            tile, piece = parted(rest, 256)
            piece = jnp.clip(piece - base, 0, pieces.shape[0] - 1)
            own = pl.ds(pl.multiple_of(row * tile_size, tile_size), tile_size)
            other = pl.ds(pl.multiple_of(block * tile_size, tile_size), tile_size)
            found = lax.dot_general(
                pieces[piece, :, other], tiles_ref[tile], (((1,), (1,)), ((), ())), preferred_element_type=jnp.float32
            )
            out_ref[:, own] += jnp.where(at < end, found, 0.0)
        return carry

    lax.fori_loop(0, (end - start + 7) // 8, some, 0)


def split_kernel(whole_ref, high_ref, low_ref):
    high = whole_ref[...].astype(jnp.bfloat16)
    high_ref[...] = high
    low_ref[...] = (whole_ref[...] - high.astype(jnp.float32)).astype(jnp.bfloat16)


def combine_kernel(links_ref, panel_ref, forward_ref, *refs):
    term_refs, (out_ref, high_ref, low_ref) = refs[:-3], refs[-3:]
    out = (links_ref[...] - 1.0) * panel_ref[...] + forward_ref[...]
    for ref in term_refs:
        out = out + ref[...].astype(jnp.float32)
    out_ref[...] = out
    high = out.astype(jnp.bfloat16)
    high_ref[...] = high
    low_ref[...] = (out - high.astype(jnp.float32)).astype(jnp.bfloat16)


def factor_of(gram):
    width = gram.shape[0]
    lanes = -(-width // 128) * 128
    rows = lax.broadcasted_iota(jnp.int32, (width, lanes), 0)
    columns = lax.broadcasted_iota(jnp.int32, (width, lanes), 1)
    left = jnp.concatenate([gram, jnp.zeros((width, lanes - width), jnp.float32)], axis=1)
    right = (rows == columns).astype(jnp.float32)
    upper, inverse = [], []
    for at in range(0, width, STEP):
        spread = [jnp.broadcast_to(left[:, at + i : at + i + 1], left.shape) for i in range(STEP)]
        lefts, rights, factors = [], [], []
        for i in range(STEP):
            row, other, column = left[i : i + 1], right[i : i + 1], spread[i]
            for k in range(i):
                part = factors[k][i : i + 1]
                row = row - part * lefts[k]
                other = other - part * rights[k]
                column = column - part * factors[k]
            scale = lax.rsqrt(column[i : i + 1])
            lefts.append(row * scale)
            rights.append(other * scale)
            factors.append(column * scale)
        upper += lefts
        inverse += rights
        left, right = left[STEP:], right[STEP:]
        if at + STEP < width:
            for i in range(STEP):
                factor = factors[i][STEP:]
                left = left - factor * lefts[i]
                right = right - factor * rights[i]
    upper = jnp.concatenate(upper, axis=0)[:, :width]
    inverse = jnp.concatenate(inverse, axis=0)[:, :width]
    return jnp.where(rows[:, :width] >= columns[:, :width], upper.T, 0.0), inverse


def gram_kernel(links_ref, start_ref, first_ref, forward_ref, *refs):
    term_refs, (panels_ref, gram_ref) = refs[:-2], refs[-2:]
    width = start_ref.shape[0]
    second = links_ref[...] * first_ref[...] + forward_ref[...]
    for ref in term_refs:
        second = second + ref[...].astype(jnp.float32)
    panels_ref[:width] = start_ref[...]
    panels_ref[width : 2 * width] = first_ref[...]
    panels_ref[2 * width :] = second
    gram = product_t(panels_ref[...], panels_ref[...])

    def block(row, column):
        return gram[row * width : (row + 1) * width, column * width : (column + 1) * width]

    gram_ref[:width] = jnp.concatenate([block(0, 0), block(1, 0), block(1, 1), block(2, 0)], axis=1)
    half = width // 2
    others = [part for of in (block(2, 1), block(2, 2)) for part in (of[:half], of[half:])]
    gram_ref[width:] = jnp.concatenate(others, axis=1)


def last_kernel(gram_ref, panels_ref, out_ref, couplings_ref, factors_ref, *, scale):
    width = out_ref.shape[0]
    def sent(place):
        return gram_ref[:width, place * width : (place + 1) * width]

    def halves(place):
        return jnp.concatenate([gram_ref[width:, at * width : (at + 1) * width] for at in (place, place + 1)], axis=0)

    gram = jnp.concatenate(
        [
            jnp.concatenate([sent(0), sent(1).T, sent(3).T], axis=1),
            jnp.concatenate([sent(1), sent(2), halves(0).T], axis=1),
            jnp.concatenate([sent(3), halves(0), halves(2)], axis=1),
        ],
        axis=0,
    )
    factor, inverse = factor_of(gram)
    out_ref[...] = product(inverse[2 * width :] * scale, panels_ref[...])

    def block(of, row, column):
        return of[row * width : (row + 1) * width, column * width : (column + 1) * width]

    rows = lax.broadcasted_iota(jnp.int32, (width, width), 0)
    columns = lax.broadcasted_iota(jnp.int32, (width, width), 1)
    unit = (rows == columns).astype(jnp.float32)
    couplings_ref[0] = product(block(inverse, 0, 0), block(factor, 1, 0)).T + unit
    turned = product(block(inverse, 1, 0), block(factor, 1, 1)) + product(block(inverse, 1, 1), block(factor, 2, 1))
    couplings_ref[1] = turned.T
    factors_ref[0] = jnp.where(rows >= columns, product(block(inverse, 0, 0), block(factor, 1, 1)), 0.0)
    factors_ref[1] = jnp.where(rows >= columns, product(block(inverse, 1, 1), block(factor, 2, 2)), 0.0)


def room_for(*arrays):
    return (2 << 20) + sum(math.prod(array.shape) * jnp.dtype(array.dtype).itemsize for array in arrays)


def call(kernel, out, *args, name, scratch=(), specs=None, cost=None):
    return pl.pallas_call(
        kernel,
        out_shape=out,
        in_specs=specs or [VMEM] * len(args),
        out_specs=jax.tree.map(lambda _: VMEM, out),
        scratch_shapes=list(scratch),
        compiler_params=pltpu.CompilerParams(vmem_limit_bytes=room_for(*args, *jax.tree.leaves(out), *scratch)),
        cost_estimate=cost,
        name=name,
    )(*args)


def on_device(tile_values, tile_rows, tile_slots, send_list, self_links, start_panel):
    count = lax.axis_size("rows")
    width, here = start_panel.shape
    tiles, tile_size, _ = tile_values.shape
    capacity = send_list.shape[2]
    f32, bf16 = jnp.float32, jnp.bfloat16
    shape = jax.ShapeDtypeStruct
    links = self_links[None, :]
    me = lax.axis_index("rows").astype(jnp.int32).reshape(1)
    panel = shape((width, here), f32)
    half = shape((width, here), bf16)
    cost = pl.CostEstimate(flops=2 * tiles * width * tile_size * tile_size, bytes_accessed=1 << 10, transcendentals=0)

    def first_products(token):
        return pl.pallas_call(
            products_kernel,
            out_shape=(shape((tiles, width, tile_size), f32), pltpu.VMEM(tile_values.shape, bf16), half, half),
            in_specs=[SMEM, ANY, ANY, ANY],
            out_specs=(VMEM,) * 4,
            scratch_shapes=[pltpu.VMEM((width, here), f32), pltpu.SemaphoreType.DMA((tiles // UNROLL + 1,))],
            compiler_params=pltpu.CompilerParams(vmem_limit_bytes=room_for(tile_values, panel, panel, shape((tiles, width, tile_size), f32))),
            cost_estimate=cost,
            name="products",
        )(
            tile_rows, pltpu.with_memory_space_constraint(start_panel, pltpu.HBM),
            pltpu.with_memory_space_constraint(tile_values, pltpu.HBM), token,
        )

    lists, list_place, (products, held, high, low) = gather_lists(send_list.reshape(1, -1), first_products)
    orders = gather_orders(count)
    order = [offset for group in orders for offsets in group for offset in offsets]
    gathered_place = np.argsort(np.array(order)).astype(np.int32)
    early_pieces = sum(map(len, orders[0]))
    fixed = jnp.concatenate(
        [me, jnp.asarray(positions(count)), jnp.asarray(list_place), tile_rows, tile_slots, jnp.asarray(gathered_place)]
    )
    indices = (fixed, lists)
    sizes = (count, capacity, tiles, tile_size)
    spec = [SMEM] * len(indices)
    total_type = f32 if count <= 16 else bf16

    sums = (shape((count // 2, width, here), total_type), shape((count // 2, width, here), bf16))
    scratch = [pltpu.VMEM((count, width, here), total_type)]

    def first_sums(token):
        return call(
            functools.partial(sums_kernel, sizes=sizes), sums, *indices, products, token,
            name="sums", specs=spec + [VMEM, ANY], scratch=scratch, cost=cost,
        )

    def backward(high, low, token):
        return call(
            functools.partial(backward_kernel, sizes=sizes), sums, *indices, high, low, held,
            name="backward", specs=spec + [VMEM] * 3, scratch=scratch, cost=cost,
        )

    plan = pl.pallas_call(
        functools.partial(plan_kernel, sizes=sizes, early=early_pieces),
        out_shape=shape((tiles + 1,), jnp.int32), in_specs=spec, out_specs=SMEM, name="plan",
        compiler_params=pltpu.CompilerParams(vmem_limit_bytes=1 << 20),
    )(*indices)

    def forward(groups, base, before):
        late = before is not None
        return call(
            functools.partial(forward_kernel, groups=len(groups), base=base, late=late),
            shape((width, here), f32),
            plan, held, *groups, *([before] if late else []),
            name="late" if late else "early", specs=[SMEM] + [VMEM] * (1 + len(groups) + late),
            scratch=[pltpu.VMEM((sum(group.shape[0] for group in groups), width, here), bf16)], cost=cost,
        )

    def applied(high, sums):
        near = swap(high, 1 << stages(count)[0][-1])
        kept, over_x, over_z = reduce_panels(*sums(high))
        terms = finish_panels(kept, over_x, over_z)
        return [gather_panels(high, near, (kept, kept), forward)] + terms

    terms = applied(high, first_sums)
    first, high, low = call(combine_kernel, (panel, half, half), links, start_panel, *terms, name="combine")
    terms = applied(high, functools.partial(backward, high, low))
    all_panels = (ITERS + 1) * width
    panels, gram = call(
        gram_kernel, (shape((all_panels, here), f32), shape((width + width // 2, 4 * width), f32)), links, start_panel, first, *terms, name="gram"
    )
    both = shape((ITERS, width, width), f32)
    return call(
        functools.partial(last_kernel, scale=math.sqrt(here * count)), (panel, both, both), reduce_small(gram), panels, name="last"
    )


def solution(mesh):
    placed = (
        P(("groups", "rows"), None, None),
        P(("groups", "rows")),
        P(("groups", "rows")),
        P(("groups", "rows"), None, None),
        P(("groups", "rows")),
        P(None, ("groups", "rows")),
    )
    return jax.shard_map(
        on_device,
        mesh=mesh,
        in_specs=placed,
        out_specs=(P(None, ("groups", "rows")), P("groups", None, None), P("groups", None, None)),
        check_vma=False,
    )
```
